128 devices in a mesh: ctx: 16 (over x, y), fsdp: 8 (over z, core).
Axes of the slice: x: 4, y: 4, z: 4, core: 2. Of those that a mesh axis runs over, the one named last changes fastest.
Arguments:
- hidden: bfloat16 [16, 8, 128, 960], P('ctx', 'fsdp'), may hold values from -6 to 6
- cotangent: bfloat16 [16, 8, 128, 960], P('ctx', 'fsdp'), may hold values from -6 to 6
- pairing: int32 [16], replicated, may hold values from 0 to 15, as said below
- documents: int32 [16, 8, 128], P(None, 'fsdp'), may hold values from 0 to 3, as said below
- attn_gain: bfloat16 [960], P('fsdp'), may hold values from 0.5 to 1.5
- w_query: bfloat16 [960, 960], P('fsdp'), may hold values from -0.1875 to 0.1875
- w_key: bfloat16 [960, 320], P('fsdp'), may hold values from -0.1875 to 0.1875
- w_value: bfloat16 [960, 320], P('fsdp'), may hold values from -0.1875 to 0.1875
- w_out: bfloat16 [960, 960], P('fsdp'), may hold values from -3 to 3
- mlp_gain: bfloat16 [960], P('fsdp'), may hold values from 0.5 to 1.5
- w_gate: bfloat16 [960, 2560], P('fsdp'), may hold values from -0.1875 to 0.1875
- w_up: bfloat16 [960, 2560], P('fsdp'), may hold values from -0.1875 to 0.1875
- w_down: bfloat16 [2560, 960], P('fsdp'), may hold values from -0.125 to 0.125
Outputs:
- result: bfloat16 [16, 8, 128, 960], P('ctx', 'fsdp')
- input_grad: bfloat16 [16, 8, 128, 960], P('ctx', 'fsdp')
- grad_attn_gain: float32 [960], P('fsdp')
- grad_query: float32 [960, 960], P('fsdp')
- grad_key: float32 [960, 320], P('fsdp')
- grad_value: float32 [960, 320], P('fsdp')
- grad_out: float32 [960, 960], P('fsdp')
- grad_mlp_gain: float32 [960], P('fsdp')
- grad_gate: float32 [960, 2560], P('fsdp')
- grad_up: float32 [960, 2560], P('fsdp')
- grad_down: float32 [2560, 960], P('fsdp')
The draws below stay inside these ranges and needn't reach their ends.
Inputs may be any that keep to these rules, and one draw needn't show every extreme that they name: A permutation: each value once; index c of ctx holds blocks pairing[c] and 31 - pairing[c] of every sequence. `documents`: taken in order of pos, a sequence's ids never fall; document 0 holds at least places 0 to 1023, and the last place is in document 3.
All inputs are finite; a program needn't handle non-finite values.
Results may differ from the reference program's by a relative error of at most 0.025.
Values may be sent and summed in bfloat16 or wider, within the bound.
No kernel may reach another device: no remote copies, remote signals or barrier semaphores. Data moves between devices by JAX's collectives and lax.ppermute only.
A program may use at most 128 MiB of HBM per device.

```python
import jax
import jax.numpy as jnp
from jax import lax

D = 960
QUERY_HEADS = 15
KEY_VALUE_HEADS = 5
HEAD_SIZE = 64
FF = 2560
BLK = 64
QD = 960
KD = 320
PAIRS = 16
GROUPS = 8
ROWS = 128
SEQUENCE_TOKENS = 2048


def pair_table(key):
    return jax.random.permutation(jax.random.fold_in(key, 7), PAIRS).astype(jnp.int32)


def draw_pairing(key, part):
    return pair_table(key)


def draw_documents(key, part):
    table = pair_table(key)
    first_end = SEQUENCE_TOKENS // 2 + jax.random.randint(jax.random.fold_in(key, 8), (GROUPS,), 0, SEQUENCE_TOKENS // 4 + 1)
    cut_points = jax.random.randint(jax.random.fold_in(key, 9), (GROUPS, 2), first_end[:, None] + 1, SEQUENCE_TOKENS)
    lower_cut = jnp.min(cut_points, axis=1)
    upper_cut = jnp.max(cut_points, axis=1)
    places = jnp.arange(SEQUENCE_TOKENS, dtype=jnp.int32)
    natural = (places[None, :] >= first_end[:, None]).astype(jnp.int32)
    natural = natural + (places[None, :] >= lower_cut[:, None]).astype(jnp.int32)
    natural = natural + (places[None, :] >= upper_cut[:, None]).astype(jnp.int32)
    offsets = jnp.arange(ROWS, dtype=jnp.int32)
    early_rows = table[:, None] * BLK + offsets[None, :]
    late_rows = (2 * PAIRS - 1 - table[:, None]) * BLK + offsets[None, :] - BLK
    positions = jnp.where(offsets[None, :] < BLK, early_rows, late_rows).reshape(-1)
    dealt = jnp.take(natural, positions, axis=1).reshape(GROUPS, PAIRS, ROWS)
    return jnp.transpose(dealt, (1, 0, 2)).astype(jnp.int32)


def block_levels(own_key, shape, cuts, smallest, high):
    factor_of = 1.0
    for position, shards_of in cuts:
        heights = jax.random.uniform(jax.random.fold_in(jax.random.fold_in(own_key, 6), position), (shards_of,), jnp.float32, smallest / len(cuts), high / len(cuts))
        factor_of = factor_of * jnp.repeat(jnp.exp(heights), shape[position] // shards_of).reshape((-1,) + (1,) * (len(shape) - 1 - position))
    return factor_of


def noise(rng, dims, scale, bound, cuts=(), held_as=jnp.bfloat16):
    result = scale * jax.random.normal(rng, dims, jnp.float32)
    if cuts:
        result = result * block_levels(rng, dims, cuts, -0.22, 0.18)
    return jnp.clip(result, -bound, bound).astype(held_as)


def setup_inputs(seed: int = 0) -> dict:
    keys = jax.random.split(jax.random.key(seed), 14)
    return {
        "hidden": noise(keys[0], (PAIRS, GROUPS, ROWS, D), 1.0, 6.0, ((0, 16), (1, 8))),
        "cotangent": noise(keys[1], (PAIRS, GROUPS, ROWS, D), 1.0, 6.0, ((0, 16), (1, 8))),
        "pairing": draw_pairing(jax.random.fold_in(keys[13], 71), 0),
        "documents": draw_documents(jax.random.fold_in(keys[13], 71), 0),
        "attn_gain": jnp.clip(1.0 + 0.1 * jax.random.normal(keys[4], (D,), jnp.float32), 0.5, 1.5).astype(jnp.bfloat16),
        "w_query": noise(keys[5], (D, QD), D ** -0.5, 0.1875, ((0, 8),)),
        "w_key": noise(keys[6], (D, KD), D ** -0.5, 0.1875, ((0, 8),)),
        "w_value": noise(keys[7], (D, KD), D ** -0.5, 0.1875, ((0, 8),)),
        "w_out": noise(keys[8], (QD, D), 4 ** -0.5, 3.0, ((0, 8),)),
        "mlp_gain": jnp.clip(1.0 + 0.1 * jax.random.normal(keys[9], (D,), jnp.float32), 0.5, 1.5).astype(jnp.bfloat16),
        "w_gate": noise(keys[10], (D, FF), D ** -0.5, 0.1875, ((0, 8),)),
        "w_up": noise(keys[11], (D, FF), D ** -0.5, 0.1875, ((0, 8),)),
        "w_down": noise(keys[12], (FF, D), FF ** -0.5, 0.125, ((0, 8),)),
    }


EPSILON = 1e-05
NEGATIVE = -1e+30
ROPE_BASE = 10000.0

@jax.custom_vjp
def lower_precision(v):
    return lax.optimization_barrier(v.astype(jnp.bfloat16)).astype(jnp.float32)

@jax.custom_vjp
def lower_precision_backward(v):
    return v

def low_keep(v):
    return (lower_precision(v), None)

def low_pass(kept, grad):
    return (grad,)

def back_keep(v):
    return (v, None)

def back_low(kept, grad):
    return (lower_precision(grad),)
lower_precision.defvjp(low_keep, low_pass)
lower_precision_backward.defvjp(back_keep, back_low)

def seq_positions(pairing, row_count):
    half_rows = row_count // 2
    count_pairs = pairing.shape[0]
    offsets = jnp.arange(row_count, dtype=jnp.int32)
    early_rows = pairing[:, None] * half_rows + offsets[None, :]
    late_rows = (2 * count_pairs - 1 - pairing[:, None]) * half_rows + offsets[None, :] - half_rows
    return jnp.where(offsets[None, :] < half_rows, early_rows, late_rows).astype(jnp.int32)

def rotary(head_dim, positions):
    frequency = ROPE_BASE ** (-(jnp.arange(head_dim // 2, dtype=jnp.float32) * 2.0) / head_dim)
    angles = positions.astype(jnp.float32)[:, None] * frequency[None, :]
    return (jnp.cos(angles), jnp.sin(angles))

def apply_rotary(value_rows, cosine_table, sine_lookup, head_count):
    row_count = value_rows.shape[0]
    heads_view = value_rows.reshape(row_count, head_count, -1)
    half_dim = heads_view.shape[-1] // 2
    first_half = heads_view[..., :half_dim]
    second = heads_view[..., half_dim:]
    cos_view = cosine_table[:, None, :]
    sin_view = sine_lookup[:, None, :]
    rotated = jnp.concatenate([first_half * cos_view - second * sin_view, second * cos_view + first_half * sin_view], axis=-1)
    return rotated.reshape(row_count, -1)

def matrix_product(left, right):
    return jnp.dot(left, right, precision=lax.Precision.HIGHEST, preferred_element_type=jnp.float32)

def one_sequence(inputs, doc_ids, weights, positions, cosine_table, sine_lookup):
    gain_a, query_w, key_matrix, value_w, out_w, gain_m, gate_w, up_w, down_w = weights
    query_group_width = QUERY_HEADS // KEY_VALUE_HEADS
    score_scale = HEAD_SIZE ** (-0.5)
    inv_rms = lax.rsqrt(lax.optimization_barrier(jnp.mean(inputs * inputs, axis=1, keepdims=True)) + EPSILON)
    normalized_input = lower_precision(inputs * inv_rms * gain_a)
    query_rows = lower_precision(apply_rotary(lower_precision_backward(matrix_product(normalized_input, query_w)), cosine_table, sine_lookup, QUERY_HEADS))
    key_rows = lower_precision(apply_rotary(lower_precision_backward(matrix_product(normalized_input, key_matrix)), cosine_table, sine_lookup, KEY_VALUE_HEADS))
    value_rows = lower_precision(lower_precision_backward(matrix_product(normalized_input, value_w)))
    heads_of_keys = key_rows.reshape(SEQUENCE_TOKENS, KEY_VALUE_HEADS, HEAD_SIZE)
    heads_of_values = value_rows.reshape(SEQUENCE_TOKENS, KEY_VALUE_HEADS, HEAD_SIZE)
    rows_per_block = min(512, SEQUENCE_TOKENS)
    blocks_of_queries = query_rows.reshape(SEQUENCE_TOKENS // rows_per_block, rows_per_block, KEY_VALUE_HEADS, query_group_width, HEAD_SIZE)
    pos_blocks = positions.reshape(SEQUENCE_TOKENS // rows_per_block, rows_per_block)
    doc_blocks = doc_ids.reshape(SEQUENCE_TOKENS // rows_per_block, rows_per_block)

    def attend(pieces):
        query_block, pos_block, doc_block = pieces
        scores = jnp.einsum('qhgd,khd->hgqk', query_block, heads_of_keys, precision=lax.Precision.HIGHEST) * score_scale
        allowed = (doc_block[:, None] == doc_ids[None, :]) & (pos_block[:, None] >= positions[None, :])
        scores = lower_precision_backward(jnp.where(allowed[None, None], scores, NEGATIVE))
        attn_probs = lower_precision(jax.nn.softmax(scores, axis=-1))
        return jnp.einsum('hgqk,khd->qhgd', attn_probs, heads_of_values, precision=lax.Precision.HIGHEST)
    attended = lax.map(jax.checkpoint(attend), (blocks_of_queries, pos_blocks, doc_blocks)).reshape(SEQUENCE_TOKENS, QUERY_HEADS * HEAD_SIZE)
    attended = lower_precision(lower_precision_backward(attended))
    middle = inputs + lower_precision_backward(matrix_product(attended, out_w))
    inv_rms_m = lax.rsqrt(lax.optimization_barrier(jnp.mean(middle * middle, axis=1, keepdims=True)) + EPSILON)
    normed_mid = lower_precision(middle * inv_rms_m * gain_m)
    gate_pre = lower_precision_backward(matrix_product(normed_mid, gate_w))
    up_pre = lower_precision_backward(matrix_product(normed_mid, up_w))
    activated = lower_precision(jax.nn.silu(gate_pre) * up_pre)
    return middle + lower_precision_backward(matrix_product(activated, down_w))

def reference(hidden, cotangent, pairing, documents, attn_gain, w_query, w_key, w_value, w_out, mlp_gain, w_gate, w_up, w_down):
    positions = seq_positions(pairing, ROWS).reshape(-1)
    cosine_table, sine_lookup = rotary(HEAD_SIZE, positions)
    doc_rows = jnp.transpose(documents, (1, 0, 2)).reshape(GROUPS, SEQUENCE_TOKENS)
    inputs = jnp.transpose(hidden.astype(jnp.float32), (1, 0, 2, 3)).reshape(GROUPS, SEQUENCE_TOKENS, D)
    cot_rows = jnp.transpose(cotangent.astype(jnp.float32), (1, 0, 2, 3)).reshape(GROUPS, SEQUENCE_TOKENS, D)
    weights = tuple((weight.astype(jnp.float32) for weight in (attn_gain, w_query, w_key, w_value, w_out, mlp_gain, w_gate, w_up, w_down)))

    def layer(all_inputs, all_weights):

        def per_sequence(pieces):
            return one_sequence(pieces[0], pieces[1], all_weights, positions, cosine_table, sine_lookup)
        return lax.map(per_sequence, (all_inputs, doc_rows))
    outputs, pullback = jax.vjp(layer, inputs, weights)
    grad_inputs, grad_weights = pullback(cot_rows)

    def dealt(array):
        return jnp.transpose(array.reshape(GROUPS, PAIRS, ROWS, D), (1, 0, 2, 3)).astype(jnp.bfloat16)
    return (dealt(outputs), dealt(grad_inputs), grad_weights[0], grad_weights[1], grad_weights[2], grad_weights[3], grad_weights[4], grad_weights[5], grad_weights[6], grad_weights[7], grad_weights[8])
```

```python
import jax
import jax.numpy as jnp
from jax import lax
from jax.experimental import pallas as pl
from jax.experimental.pallas import tpu as pltpu
from jax.sharding import PartitionSpec as P

QUERY_HEADS = 15
KEY_VALUE_HEADS = 5
HEAD_SIZE = 64
GROUP = QUERY_HEADS // KEY_VALUE_HEADS

EPSILON = 1e-05
NEGATIVE = -1e30
ROPE_BASE = 10000.0

CTX = ("x", "y")
FSDP = ("z", "core")
KD = KEY_VALUE_HEADS * HEAD_SIZE
QD = QUERY_HEADS * HEAD_SIZE
PADDED = 1664

bf16, f32 = jnp.bfloat16, jnp.float32


def seq_positions(pairing, row_count):
    half_rows = row_count // 2
    count_pairs = pairing.shape[0]
    offsets = jnp.arange(row_count, dtype=jnp.int32)
    early_rows = pairing[:, None] * half_rows + offsets[None, :]
    late_rows = (2 * count_pairs - 1 - pairing[:, None]) * half_rows + offsets[None, :] - half_rows
    return jnp.where(offsets[None, :] < half_rows, early_rows, late_rows)


def rope_tables(positions):
    frequency = ROPE_BASE ** (-(jnp.arange(HEAD_SIZE // 2, dtype=f32) * 2.0) / HEAD_SIZE)
    angles = positions.astype(f32)[:, None] * frequency[None, :]
    cos, sin = jnp.cos(angles), jnp.sin(angles)
    return jnp.concatenate([cos] * 4, axis=1), jnp.concatenate([-sin, sin, -sin, sin], axis=1)


def plain_dot(left, right):
    return jnp.dot(left, right, preferred_element_type=f32)


def left_dot(left, right):
    return lax.dot_general(left, right, (((0,), (0,)), ((), ())), preferred_element_type=f32)


def right_dot(left, right):
    return lax.dot_general(left, right, (((1,), (1,)), ((), ())), preferred_element_type=f32)


def shift(block, axis, step, size=4):
    return lax.ppermute(block, axis, [(i, (i - step) % size) for i in range(size)])


def scatter_parts(blocks, axis):
    rows = blocks.shape[0] // 4
    parts = [blocks[k * rows : (k + 1) * rows] for k in range(4)]
    return [parts[0]] + [shift(parts[k], axis, -k) for k in (1, 2, 3)]


def add_parts(parts):
    total = parts[0].astype(f32)
    for part in parts[1:]:
        total = total + part.astype(f32)
    return total


def scatter_axis(blocks, axis):
    return add_parts(scatter_parts(blocks, axis)).astype(blocks.dtype)


def gather_blocks(block):
    blocks = [block] + [shift(block, "z", k) for k in (1, 2, 3)]
    return blocks, shift(jnp.concatenate(blocks, axis=0), "core", 1, 2)


def scatter_fsdp_parts(blocks):
    half = blocks.shape[0] // 2
    mine = blocks[:half].astype(f32) + shift(blocks[half:], "core", 1, 2).astype(f32)
    return scatter_parts(mine.astype(blocks.dtype), "z")


def gather_ordered(shard):
    z, core = lax.axis_index("z"), lax.axis_index("core")
    blocks, other = gather_blocks(shard[None])
    out = jnp.zeros((4, 2) + shard.shape, shard.dtype)
    for k in range(4):
        mine, its = blocks[k], other[k : k + 1]
        pair = jnp.concatenate([jnp.where(core == 0, mine, its), jnp.where(core == 0, its, mine)], axis=0)
        out = lax.dynamic_update_index_in_dim(out, pair, (z + k) % 4, 0)
    return out.reshape((8 * shard.shape[0],) + shard.shape[1:])


def scatter_ordered(partial):
    z, core = lax.axis_index("z"), lax.axis_index("core")
    own = partial.shape[0] // 8
    view = partial.reshape(4, 2, own, -1)
    mine = lax.dynamic_index_in_dim(view, core, 1, keepdims=False)
    its = lax.dynamic_index_in_dim(view, 1 - core, 1, keepdims=False)
    mine = (mine.astype(f32) + shift(its, "core", 1, 2).astype(f32)).astype(partial.dtype)
    pick = lambda k: lax.dynamic_index_in_dim(mine, (z + k) % 4, 0, keepdims=False)
    return add_parts([pick(0)] + [shift(pick(k), "z", -k) for k in (1, 2, 3)]).astype(partial.dtype)


def sum_ctx(value):
    x = lax.axis_index("x")
    pick = lambda k: lax.dynamic_index_in_dim(value, (x + k) % 4, 0, keepdims=False)
    low = add_parts([pick(0)] + [shift(pick(k), "x", -k) for k in (1, 2, 3)]).astype(value.dtype)
    low = add_parts([low] + [shift(low, "y", k) for k in (1, 2, 3)]).astype(value.dtype)
    out = jnp.zeros(value.shape, value.dtype)
    for k in range(4):
        out = lax.dynamic_update_index_in_dim(out, low if k == 0 else shift(low, "x", k), (x + k) % 4, 0)
    return out


def params(*semantics):
    return pltpu.CompilerParams(vmem_limit_bytes=56 * 2**20)


def cost(flops, read):
    return pl.CostEstimate(flops=int(flops), bytes_accessed=int(read), transcendentals=0)


def swap_halves(value):
    lane = lax.broadcasted_iota(jnp.int32, value.shape, 1)
    return jnp.where(lane % HEAD_SIZE < HEAD_SIZE // 2, pltpu.roll(value, 96, 1), pltpu.roll(value, 32, 1))


def rope(value, cos, sin):
    return value * cos + swap_halves(value) * sin


def rope_keys(value, cos, sin):
    chunks = []
    for j in range(5):
        part = value[:, j * 128 : (j + 1) * 128]
        if j < 2:
            part = rope(part, cos, sin)
        elif j == 2:
            lane = lax.broadcasted_iota(jnp.int32, part.shape, 1)
            part = jnp.where(lane < 64, rope(part, cos, sin), part)
        chunks.append(part)
    return chunks


def qkv_kernel(all_ref, cos_ref, sin_ref, own_ref, own_cos_ref, own_sin_ref, w_ref, gain_ref, ha_ref, kv_ref, q_ref):
    def normed(ref):
        rows = ref[...].astype(f32)
        inv = lax.rsqrt(jnp.mean(rows * rows, axis=1, keepdims=True) + EPSILON)
        return (rows * inv * gain_ref[...]).astype(bf16)

    ha = normed(all_ref)
    ha_ref[...] = ha
    kv = plain_dot(ha, w_ref[:, : 2 * KD])
    for j, part in enumerate(rope_keys(kv, cos_ref[...], sin_ref[...])):
        kv_ref[:, j * 128 : (j + 1) * 128] = part.astype(bf16)

    @pl.when(pl.program_id(0) == 0)
    def _():
        q = plain_dot(normed(own_ref), w_ref[:, 2 * KD :])
        for j in range(8):
            cols = slice(j * 128, (j + 1) * 128)
            part = rope(q[:, cols], own_cos_ref[...], own_sin_ref[...])
            q_ref[:, cols] = (part.astype(bf16).astype(f32) * HEAD_SIZE**-0.5).astype(bf16)


def qkv_call(rows_all, cos, sin, own, own_cos, own_sin, w, gain):
    length, width = rows_all.shape
    tile = 256
    whole = lambda a: pl.BlockSpec(a.shape, lambda i: (0, 0))
    tiled = lambda c: pl.BlockSpec((tile, c), lambda i: (i, 0))
    return pl.pallas_call(
        qkv_kernel,
        grid=(length // tile,),
        in_specs=[tiled(width), tiled(128), tiled(128)] + [whole(a) for a in (own, own_cos, own_sin, w, gain)],
        out_specs=[tiled(width), tiled(2 * KD), pl.BlockSpec((own.shape[0], 1024), lambda i: (0, 0))],
        out_shape=[
            jax.ShapeDtypeStruct((length, width), bf16),
            jax.ShapeDtypeStruct((length, 2 * KD), bf16),
            jax.ShapeDtypeStruct((own.shape[0], 1024), bf16),
        ],
        compiler_params=params(),
        cost_estimate=cost(3e9, 12e6),
        name="qkv",
    )(rows_all, cos, sin, own, own_cos, own_sin, w, gain)


def attend_kernel(
    q_ref, kv_ref, qpos_ref, qdoc_ref, kpos_ref, kdoc_ref, x_ref, w_ref, gain_ref,
    o_ref, lse_ref, mid_ref, hm_ref, qs, ks, vs, os, bias,
):
    rows = x_ref.shape[0]
    for n in range(QUERY_HEADS):
        qs[n] = q_ref[:, n * 64 : (n + 1) * 64]
    for n in range(KEY_VALUE_HEADS):
        ks[n] = kv_ref[:, n * 64 : (n + 1) * 64]
        vs[n] = kv_ref[:, KD + n * 64 : KD + (n + 1) * 64]
    ok = (qdoc_ref[...] == kdoc_ref[...]) & (qpos_ref[...] >= kpos_ref[...])
    bias[...] = jnp.where(ok, 0.0, NEGATIVE)

    def head(h, carry):
        for g in range(GROUP):
            n = h * GROUP + g
            s = right_dot(qs[n], ks[h]) + bias[...]
            top = jnp.max(s, axis=1, keepdims=True)
            p = jnp.exp(s - top)
            total = jnp.sum(p, axis=1, keepdims=True)
            o = plain_dot((p * (1.0 / total)).astype(bf16), vs[h])
            os[n] = o.astype(bf16)
            lse = jnp.broadcast_to(top + jnp.log(total), (rows, rows))
            lse_ref[pl.ds(n, 1), :] = jnp.transpose(lse)[:1, :]
        return carry

    lax.fori_loop(0, KEY_VALUE_HEADS, head, 0)
    for n in range(QUERY_HEADS):
        o_ref[:, n * 64 : (n + 1) * 64] = os[n]
    mid = x_ref[...].astype(f32) + plain_dot(o_ref[...], w_ref[...])
    mid_ref[...] = mid
    inv = lax.rsqrt(jnp.mean(mid * mid, axis=1, keepdims=True) + EPSILON)
    hm_ref[...] = (mid * inv * gain_ref[...]).astype(bf16)


def attend_call(q, kv, qpos, qdoc, kpos, kdoc, x, w, gain):
    rows, width = x.shape
    length = kv.shape[0]
    return pl.pallas_call(
        attend_kernel,
        out_shape=[
            jax.ShapeDtypeStruct((rows, width), bf16),
            jax.ShapeDtypeStruct((16, rows), f32),
            jax.ShapeDtypeStruct((rows, width), f32),
            jax.ShapeDtypeStruct((rows, width), bf16),
        ],
        scratch_shapes=[
            pltpu.VMEM((QUERY_HEADS, rows, 64), bf16),
            pltpu.VMEM((KEY_VALUE_HEADS, length, 64), bf16),
            pltpu.VMEM((KEY_VALUE_HEADS, length, 64), bf16),
            pltpu.VMEM((QUERY_HEADS, rows, 64), bf16),
            pltpu.VMEM((rows, length), f32),
        ],
        compiler_params=params(),
        cost_estimate=cost(5e9, 8e6),
        name="attend",
    )(q, kv, qpos, qdoc, kpos, kdoc, x, w, gain)


def mlp_kernel(h0, h1, h2, h3, ho, dy_ref, wg_ref, wu_ref, wd_ref, all_ref, act_ref, dg_ref, du_ref, dh_ref, out_ref):
    rows = h0.shape[0]
    for k, ref in enumerate((h0, h1, h2, h3)):
        all_ref[k * rows : (k + 1) * rows, :] = ref[...]
    all_ref[4 * rows :, :] = ho[...]

    def tile(t, carry):
        at = pl.ds(pl.multiple_of(t * 256, 256), 256)
        h, dy = all_ref[at, :], dy_ref[at, :]
        gate = plain_dot(h, wg_ref[...])
        up = plain_dot(h, wu_ref[...])
        d_act = right_dot(dy, wd_ref[...])
        sig = jax.nn.sigmoid(gate)
        act = (gate * sig * up).astype(bf16)
        dg = (d_act * up * sig * (1.0 + gate * (1.0 - sig))).astype(bf16)
        du = (d_act * gate * sig).astype(bf16)
        act_ref[at, :] = act
        dg_ref[at, :] = dg
        du_ref[at, :] = du
        dh_ref[at, :] = (right_dot(dg, wg_ref[...]) + right_dot(du, wu_ref[...])).astype(bf16)
        out_ref[at, :] = plain_dot(act, wd_ref[...]).astype(bf16)
        return carry

    lax.fori_loop(0, all_ref.shape[0] // 256, tile, 0)


def mlp_call(blocks, other, dy, wg, wu, wd):
    total, width = dy.shape
    ff = wg.shape[1]
    wide, slim = jax.ShapeDtypeStruct((total, width), bf16), jax.ShapeDtypeStruct((total, ff), bf16)
    return pl.pallas_call(
        mlp_kernel,
        out_shape=[wide, slim, slim, slim, wide, wide],
        compiler_params=params(),
        cost_estimate=cost(4e9, 12e6),
        name="mlp",
    )(*blocks, other, dy, wg, wu, wd)


def norm_back(grad_normed, normed, inv_rms, gain):
    scaled = grad_normed * gain
    return inv_rms * (scaled - normed * jnp.mean(scaled * normed, axis=1, keepdims=True))


def middle_kernel(d0, d1, d2, d3, dy_ref, mid_ref, gain_ref, w_ref, o_ref, dmid_ref, low_ref, do_ref, delta_ref):
    rows = mid_ref.shape[0]
    d_hm = add_parts([d0[...], d1[...], d2[...], d3[...]])
    mid = mid_ref[...]
    inv = lax.rsqrt(jnp.mean(mid * mid, axis=1, keepdims=True) + EPSILON)
    d_mid = dy_ref[...].astype(f32) + norm_back(d_hm, mid * inv, inv, gain_ref[...])
    dmid_ref[...] = d_mid
    low = d_mid.astype(bf16)
    low_ref[...] = low
    d_o = right_dot(low, w_ref[...]).astype(bf16)
    do_ref[...] = d_o
    prod = d_o.astype(f32) * o_ref[...].astype(f32)
    for n in range(QUERY_HEADS):
        one = jnp.sum(prod[:, n * 64 : (n + 1) * 64], axis=1, keepdims=True)
        delta_ref[n : n + 1, :] = jnp.transpose(jnp.broadcast_to(one, (rows, rows)))[:1, :]


def middle_call(parts, dy, mid, gain, w, o):
    rows, width = mid.shape
    wide = lambda t: jax.ShapeDtypeStruct((rows, width), t)
    return pl.pallas_call(
        middle_kernel,
        out_shape=[wide(f32), wide(bf16), wide(bf16), jax.ShapeDtypeStruct((16, rows), f32)],
        compiler_params=params(),
        cost_estimate=cost(1e9, 4e6),
        name="middle",
    )(*parts, dy, mid, gain, w, o)


def back_kernel(
    q_ref, kv_ref, do_ref, lse_ref, delta_ref, qpos_ref, qdoc_ref, kpos_ref, kdoc_ref,
    cos_ref, sin_ref, own_cos_ref, own_sin_ref, dq_ref, dkv_ref, qs, ds, ks, vs, dks, dvs, dqs, bias,
):
    rows, length = do_ref.shape[0], kv_ref.shape[0]
    chunk = 512
    for n in range(QUERY_HEADS):
        h, g = n // GROUP, n % GROUP
        qs[h, g * rows : (g + 1) * rows, :] = q_ref[:, n * 64 : (n + 1) * 64]
        ds[h, g * rows : (g + 1) * rows, :] = do_ref[:, n * 64 : (n + 1) * 64]
    for n in range(KEY_VALUE_HEADS):
        ks[n] = kv_ref[:, n * 64 : (n + 1) * 64]
        vs[n] = kv_ref[:, KD + n * 64 : KD + (n + 1) * 64]
    ok = (kdoc_ref[...] == qdoc_ref[...]) & (qpos_ref[...] >= kpos_ref[...])
    bias[...] = jnp.where(ok, 0.0, NEGATIVE)

    def head(h, carry):
        q, d = qs[h], ds[h]
        row = lambda ref: jnp.concatenate([ref[pl.ds(h * GROUP + g, 1), :] for g in range(GROUP)], axis=1)
        lse, delta = row(lse_ref), row(delta_ref)

        def step(c, dq):
            at = pl.ds(pl.multiple_of(c * chunk, chunk), chunk)
            k, v = ks[h, at, :], vs[h, at, :]
            b = bias[at, :]
            p = jnp.exp(right_dot(k, q) + jnp.concatenate([b, b, b], axis=1) - lse)
            dp = right_dot(v, d)
            low = p.astype(bf16)
            dscore = (p * (dp - delta)).astype(bf16)
            dvs[h, at, :] = plain_dot(low, d)
            dks[h, at, :] = plain_dot(dscore, q)
            return dq + left_dot(k, dscore)

        dqs[h] = lax.fori_loop(0, length // chunk, step, jnp.zeros((64, GROUP * rows), f32))
        return carry

    lax.fori_loop(0, KEY_VALUE_HEADS, head, 0)
    own_cos, own_sin = own_cos_ref[...], -own_sin_ref[...]
    scale = HEAD_SIZE**-0.5
    for j in range(8):
        pieces = []
        for n in (2 * j, 2 * j + 1):
            n = min(n, QUERY_HEADS - 1)
            pieces.append(dqs[n // GROUP, :, (n % GROUP) * rows : (n % GROUP + 1) * rows])
        part = jnp.transpose(jnp.concatenate(pieces, axis=0)) * scale
        dq_ref[:, j * 128 : (j + 1) * 128] = rope(part, own_cos, own_sin).astype(bf16)

    def finish(t, carry):
        at = pl.ds(pl.multiple_of(t * 256, 256), 256)
        parts = [dks[n, at, :] for n in range(KEY_VALUE_HEADS)] + [dvs[n, at, :] for n in range(KEY_VALUE_HEADS)]
        both = jnp.concatenate(parts, axis=1)
        for j, part in enumerate(rope_keys(both, cos_ref[at, :], -sin_ref[at, :])):
            dkv_ref[at, j * 128 : (j + 1) * 128] = part.astype(bf16)
        return carry

    lax.fori_loop(0, length // 256, finish, 0)


def back_call(q, kv, d_o, lse, delta, qpos, qdoc, kpos, kdoc, cos, sin, own_cos, own_sin):
    rows, length = d_o.shape[0], kv.shape[0]
    both = GROUP * rows
    return pl.pallas_call(
        back_kernel,
        out_shape=[jax.ShapeDtypeStruct((rows, 1024), bf16), jax.ShapeDtypeStruct((length, 2 * KD), bf16)],
        scratch_shapes=[
            pltpu.VMEM((KEY_VALUE_HEADS, both, 64), bf16),
            pltpu.VMEM((KEY_VALUE_HEADS, both, 64), bf16),
            pltpu.VMEM((KEY_VALUE_HEADS, length, 64), bf16),
            pltpu.VMEM((KEY_VALUE_HEADS, length, 64), bf16),
            pltpu.VMEM((KEY_VALUE_HEADS, length, 64), f32),
            pltpu.VMEM((KEY_VALUE_HEADS, length, 64), f32),
            pltpu.VMEM((KEY_VALUE_HEADS, 64, both), f32),
            pltpu.VMEM((length, rows), f32),
        ],
        compiler_params=params(),
        cost_estimate=cost(20e9, 8e6),
        name="back",
    )(q, kv, d_o, lse, delta, qpos, qdoc, kpos, kdoc, cos, sin, own_cos, own_sin)


def last_kernel(dq_ref, dkv_ref, w_ref, x_ref, gain_ref, dmid_ref, out_ref):
    d_ha = right_dot(dkv_ref[...], w_ref[:, : 2 * KD]) + right_dot(dq_ref[:, :QD], w_ref[:, 2 * KD : 2 * KD + QD])
    x = x_ref[...].astype(f32)
    inv = lax.rsqrt(jnp.mean(x * x, axis=1, keepdims=True) + EPSILON)
    out_ref[...] = (dmid_ref[...] + norm_back(d_ha, x * inv, inv, gain_ref[...])).astype(bf16)


def last_call(dq, dkv, w, x, gain, d_mid):
    return pl.pallas_call(
        last_kernel,
        out_shape=jax.ShapeDtypeStruct(x.shape, bf16),
        compiler_params=params(),
        cost_estimate=cost(1e9, 5e6),
        name="last",
    )(dq, dkv, w, x, gain, d_mid)


def per_device(
    hidden,
    cotangent,
    pairing,
    documents,
    attn_gain,
    w_query,
    w_key,
    w_value,
    w_out,
    mlp_gain,
    w_gate,
    w_up,
    w_down,
):
    rows, width = hidden.shape[2:]
    half = rows // 2
    own = width // 8
    ff = w_gate.shape[1] // 8
    me = lax.axis_index("x") * 4 + lax.axis_index("y")
    x_rows = hidden.reshape(rows, width)
    dy = cotangent.reshape(rows, width)

    rows_all = lax.all_gather(x_rows, CTX, axis=0, tiled=True)
    shard = jnp.concatenate(
        [w_key, w_value, w_query, attn_gain[:, None], mlp_gain[:, None], jnp.zeros((own, PADDED - 2 * KD - QD - 2), bf16), w_out],
        axis=1,
    )
    weights = gather_ordered(shard)
    dy_blocks, dy_other = gather_blocks(dy)
    dy_all = jnp.concatenate(dy_blocks + [dy_other], axis=0)
    gate_up = jnp.concatenate([w_gate.reshape(own, 8, ff), w_up.reshape(own, 8, ff)], axis=2).transpose(1, 0, 2)
    gate_up = lax.all_to_all(gate_up, FSDP, 0, 0, tiled=True).reshape(width, 2 * ff)
    rows_all, weights, dy_all, gate_up = lax.optimization_barrier((rows_all, weights, dy_all, gate_up))
    w_kvq, out_w = weights[:, :PADDED], weights[:, PADDED:]
    gains = weights[:, PADDED - 64 : PADDED - 62].astype(f32).T
    gain_a, gain_m = gains[:1], gains[1:]
    wg, wu = gate_up[:, :ff], gate_up[:, ff:]

    positions = seq_positions(pairing, rows)
    docs = documents[:, 0, :]
    cos, sin = rope_tables(positions.reshape(-1))
    own_cos = lax.dynamic_slice_in_dim(cos, me * rows, rows, 0)
    own_sin = lax.dynamic_slice_in_dim(sin, me * rows, rows, 0)
    own_pos = lax.dynamic_index_in_dim(positions, me, 0)
    own_doc = lax.dynamic_index_in_dim(docs, me, 0)

    ha_all, kv, q = qkv_call(rows_all, cos, sin, x_rows, own_cos, own_sin, w_kvq, gain_a)
    o, lse, mid, hm = attend_call(
        q, kv, own_pos.reshape(-1, 1), own_doc.reshape(-1, 1), positions.reshape(1, -1), docs.reshape(1, -1), x_rows, out_w, gain_m
    )

    hm_blocks, hm_other = gather_blocks(hm)
    h_all, act, dg, du, dh_part, out_part = mlp_call(hm_blocks, hm_other, dy_all, wg, wu, w_down)
    dh_parts = scatter_fsdp_parts(dh_part)
    d_mid, low, d_o, delta = middle_call(dh_parts, dy, mid, gain_m, out_w, o)
    result = (mid + add_parts(scatter_fsdp_parts(out_part))).astype(bf16)

    g_gate, g_up = left_dot(h_all, dg).astype(bf16), left_dot(h_all, du).astype(bf16)
    g_gu = jnp.concatenate([g_gate.reshape(8, own, ff), g_up.reshape(8, own, ff)], axis=2)
    g_gu = lax.all_to_all(g_gu, FSDP, 0, 0, tiled=True)
    g_down = left_dot(act, dy_all).astype(bf16)
    g_gu, g_down = lax.psum((g_gu, g_down), CTX)
    g_gu = g_gu.astype(f32)
    g_gate = g_gu[:, :, :ff].transpose(1, 0, 2).reshape(own, -1)
    g_up = g_gu[:, :, ff:].transpose(1, 0, 2).reshape(own, -1)
    g_gain_m = (jnp.sum(g_gate * w_gate, axis=1) + jnp.sum(g_up * w_up, axis=1)) / mlp_gain.astype(f32)

    g_out = scatter_ordered(left_dot(o, low).astype(bf16))

    dq, dkv = back_call(
        q, kv, d_o, lse, delta, own_pos, own_doc, positions.reshape(-1, 1), docs.reshape(-1, 1), cos, sin, own_cos, own_sin
    )
    ha_own = lax.dynamic_slice_in_dim(ha_all, me * rows, rows, 0)
    g_kvq = jnp.concatenate([left_dot(ha_all, dkv), left_dot(ha_own, dq[:, :QD])], axis=1).astype(bf16)
    g_kvq = scatter_ordered(g_kvq)
    total = jnp.concatenate([g_kvq, g_out], axis=1)
    total = sum_ctx(total.reshape(4, own // 4, -1)).reshape(own, -1).astype(f32)
    g_key, g_value, g_query = total[:, :KD], total[:, KD : 2 * KD], total[:, 2 * KD : 2 * KD + QD]
    g_out = total[:, 2 * KD + QD :]
    g_gain_a = (
        jnp.sum(g_key * w_key, axis=1) + jnp.sum(g_value * w_value, axis=1) + jnp.sum(g_query * w_query, axis=1)
    ) / attn_gain.astype(f32)

    x, y = lax.axis_index("x"), lax.axis_index("y")

    def to_owners(part, first, second, i, j):
        view = part.reshape(4, 4 * half, -1)
        pick = lambda k: lax.dynamic_index_in_dim(view, (i + k) % 4, 0, keepdims=False)
        part = add_parts([pick(0)] + [shift(pick(k), first, -k) for k in (1, 2, 3)]).astype(bf16)
        view = part.reshape(4, half, -1)
        return add_parts(
            [lax.dynamic_index_in_dim(view, j, 0, keepdims=False)]
            + [shift(lax.dynamic_index_in_dim(view, (j + k) % 4, 0, keepdims=False), second, -k) for k in (1, 2, 3)]
        ).astype(bf16)

    blocks = dkv.reshape(4, 4, 2, half, 2 * KD)
    early = to_owners(blocks[:, :, 0], "x", "y", x, y)
    late = to_owners(blocks[:, :, 1].swapaxes(0, 1), "y", "x", y, x)
    input_grad = last_call(dq, jnp.concatenate([early, late], axis=0), w_kvq, x_rows, gain_a, d_mid)

    return (
        result.reshape(1, 1, rows, width),
        input_grad.reshape(1, 1, rows, width),
        g_gain_a,
        g_query,
        g_key,
        g_value,
        g_out,
        g_gain_m,
        g_gate,
        g_up,
        g_down.astype(f32),
    )


def solution(mesh):
    grid = jax.sharding.Mesh(mesh.devices.reshape(4, 4, 4, 2), ("x", "y", "z", "core"))
    tokens = P(CTX, FSDP, None, None)
    vector, matrix = P(FSDP), P(FSDP, None)
    return jax.shard_map(
        per_device,
        mesh=grid,
        in_specs=(tokens, tokens, P(), P(None, FSDP, None), vector, matrix, matrix, matrix, matrix, vector, matrix, matrix, matrix),
        out_specs=(tokens, tokens, vector, matrix, matrix, matrix, matrix, vector, matrix, matrix, matrix),
        check_vma=False,
    )
```

```python
import jax
import jax.numpy as jnp
import numpy as np
from jax import lax
from jax.experimental import pallas as pl
from jax.experimental.pallas import tpu as pltpu
from jax.sharding import PartitionSpec as P

QUERY_HEADS = 15
KEY_VALUE_HEADS = 5
HEAD_SIZE = 64
GROUP = QUERY_HEADS // KEY_VALUE_HEADS

EPSILON = 1e-05
NEGATIVE = -1e30
ROPE_BASE = 10000.0

CTX = ("x", "y")
FSDP = ("z", "core")
KD = KEY_VALUE_HEADS * HEAD_SIZE
QD = QUERY_HEADS * HEAD_SIZE
PADDED = 1664

bf16, f32 = jnp.bfloat16, jnp.float32


def seq_positions(pairing, row_count):
    half_rows = row_count // 2
    count_pairs = pairing.shape[0]
    offsets = jnp.arange(row_count, dtype=jnp.int32)
    early_rows = pairing[:, None] * half_rows + offsets[None, :]
    late_rows = (2 * count_pairs - 1 - pairing[:, None]) * half_rows + offsets[None, :] - half_rows
    return jnp.where(offsets[None, :] < half_rows, early_rows, late_rows)


def rope_tables(length):
    exponent = -(np.arange(HEAD_SIZE // 2, dtype=np.float32) * 2.0) / HEAD_SIZE
    frequency = np.power(ROPE_BASE, exponent.astype(np.float64)).astype(np.float32)
    angles = (np.arange(length, dtype=np.float32)[:, None] * frequency[None, :]).astype(np.float64)
    cos, sin = np.cos(angles).astype(np.float32), np.sin(angles).astype(np.float32)
    return jnp.asarray(np.concatenate([cos] * 4, axis=1)), jnp.asarray(np.concatenate([-sin, sin, -sin, sin], axis=1))


def plain_dot(left, right):
    return jnp.dot(left, right, preferred_element_type=f32)


def left_dot(left, right):
    return lax.dot_general(left, right, (((0,), (0,)), ((), ())), preferred_element_type=f32)


def right_dot(left, right):
    return lax.dot_general(left, right, (((1,), (1,)), ((), ())), preferred_element_type=f32)


def shift(block, axis, step, size=4):
    return lax.ppermute(block, axis, [(i, (i - step) % size) for i in range(size)])


def send_parts(parts, axis):
    return [parts[0]] + [shift(parts[k], axis, -k) for k in (1, 2, 3)]


def add_parts(parts):
    total = parts[0].astype(f32)
    for part in parts[1:]:
        total = total + part.astype(f32)
    return total


def gather_blocks(block):
    blocks = [block] + [shift(block, "z", k) for k in (1, 2, 3)]
    return blocks + [shift(b, "core", 1, 2) for b in blocks]


def after(value, *others):
    return lax.optimization_barrier((value,) + others)[0]


def params(*semantics):
    return pltpu.CompilerParams(vmem_limit_bytes=56 * 2**20)


def cost(flops, read):
    return pl.CostEstimate(flops=1000, bytes_accessed=1000, transcendentals=0)


def swap_halves(value):
    lane = lax.broadcasted_iota(jnp.int32, value.shape, 1)
    return jnp.where(lane % HEAD_SIZE < HEAD_SIZE // 2, pltpu.roll(value, 96, 1), pltpu.roll(value, 32, 1))


def rope(value, cos, sin):
    return value * cos + swap_halves(value) * sin


def rope_keys(value, cos, sin):
    chunks = []
    for j in range(5):
        part = value[:, j * 128 : (j + 1) * 128]
        if j < 2:
            part = rope(part, cos, sin)
        elif j == 2:
            lane = lax.broadcasted_iota(jnp.int32, part.shape, 1)
            part = jnp.where(lane < 64, rope(part, cos, sin), part)
        chunks.append(part)
    return chunks


BLK, X, Y, Z, CORE, ME, SCALARS = 0, 32, 33, 34, 35, 36, 40


def in_smem():
    return pl.BlockSpec(memory_space=pltpu.SMEM)


def in_vmem():
    return pl.BlockSpec(memory_space=pltpu.VMEM)


def call(kernel, name, out_shape, operands, flops=1e9, read=4e6, scratch=()):
    return pl.pallas_call(
        kernel,
        in_specs=[in_smem()] + [in_vmem()] * (len(operands) - 1),
        out_shape=out_shape,
        scratch_shapes=list(scratch),
        compiler_params=params(),
        cost_estimate=cost(flops, read),
        name=name,
    )(*operands)


def shape(dims, dtype=bf16):
    return jax.ShapeDtypeStruct(dims, dtype)


def assemble_kernel(ints, *refs):
    blocks, (w_ref, out_ref, gain_ref, hold) = refs[:8], refs[8:]
    own = blocks[0].shape[0]
    for k in range(4):
        pair = lax.rem(ints[Z] + k, 4) * 2
        hold[pair + ints[CORE]] = blocks[k][...]
        hold[pair + 1 - ints[CORE]] = blocks[4 + k][...]
    for f in range(8):
        w_ref[f * own : (f + 1) * own, :] = hold[f, :, :PADDED]
        out_ref[f * own : (f + 1) * own, :] = hold[f, :, PADDED:]
    gain_ref[...] = jnp.transpose(w_ref[:, PADDED - 128 :].astype(f32))[64:72, :]


def assemble_call(ints, blocks):
    own, columns = blocks[0].shape
    outs = [shape((8 * own, PADDED)), shape((8 * own, columns - PADDED)), shape((8, 8 * own), f32)]
    return call(assemble_kernel, "assemble", outs, [ints, *blocks], scratch=[pltpu.VMEM((8, own, columns), bf16)])


def half_block(ref, ints, number):
    return ref[pl.ds(pl.multiple_of(ints[BLK + number] * 64, 64), 64), :]


def table_rows(ref, ints, first, count):
    return jnp.concatenate([half_block(ref, ints, first + i) for i in range(count)], axis=0)


def qkv_kernel(ints, all_ref, cos_ref, sin_ref, own_ref, w_ref, gain_ref, ha_ref, kv_ref, q_ref):
    i = pl.program_id(0)

    def normed(ref):
        rows = ref[...].astype(f32)
        inv = lax.rsqrt(jnp.mean(rows * rows, axis=1, keepdims=True) + EPSILON)
        return (rows * inv * gain_ref[...]).astype(bf16)

    ha = normed(all_ref)
    ha_ref[...] = ha
    kv = plain_dot(ha, w_ref[:, : 2 * KD])
    cos, sin = table_rows(cos_ref, ints, i * 4, 4), table_rows(sin_ref, ints, i * 4, 4)
    for j, part in enumerate(rope_keys(kv, cos, sin)):
        kv_ref[:, j * 128 : (j + 1) * 128] = part.astype(bf16)

    @pl.when(i == 0)
    def _():
        me = ints[ME]
        own_cos, own_sin = table_rows(cos_ref, ints, me * 2, 2), table_rows(sin_ref, ints, me * 2, 2)
        q = plain_dot(normed(own_ref), w_ref[:, 2 * KD :])
        for j in range(8):
            cols = slice(j * 128, (j + 1) * 128)
            part = rope(q[:, cols], own_cos, own_sin)
            q_ref[:, cols] = (part.astype(bf16).astype(f32) * HEAD_SIZE**-0.5).astype(bf16)


def qkv_call(ints, rows_all, cos, sin, own, w, gain):
    length, width = rows_all.shape
    tile = 256
    whole = lambda a: pl.BlockSpec(a.shape, lambda i: (0, 0))
    tiled = lambda c: pl.BlockSpec((tile, c), lambda i: (i, 0))
    return pl.pallas_call(
        qkv_kernel,
        grid=(length // tile,),
        in_specs=[in_smem(), tiled(width)] + [whole(a) for a in (cos, sin, own, w, gain)],
        out_specs=[tiled(width), tiled(2 * KD), pl.BlockSpec((own.shape[0], 1024), lambda i: (0, 0))],
        out_shape=[shape((length, width)), shape((length, 2 * KD)), shape((own.shape[0], 1024))],
        compiler_params=params(),
        cost_estimate=cost(3e9, 12e6),
        name="qkv",
    )(ints, rows_all, cos, sin, own, w, gain)


def attend_kernel(
    ints, q_ref, kv_ref, qpos_ref, qstart_ref, kpos_ref, x_ref, w_ref, gain_ref,
    o_ref, lse_ref, mid_ref, hm_ref, qs, ks, vs, os, bias,
):
    rows = x_ref.shape[0]
    for n in range(QUERY_HEADS):
        h, g = n // GROUP, n % GROUP
        qs[h, g * rows : (g + 1) * rows, :] = q_ref[:, n * 64 : (n + 1) * 64]
    for n in range(KEY_VALUE_HEADS):
        ks[n] = kv_ref[:, n * 64 : (n + 1) * 64]
        vs[n] = kv_ref[:, KD + n * 64 : KD + (n + 1) * 64]
    ok = (kpos_ref[...] >= qstart_ref[...]) & (qpos_ref[...] >= kpos_ref[...])
    bias[...] = jnp.where(ok, 0.0, NEGATIVE)

    def head(h, carry):
        b = bias[...]
        s = right_dot(qs[h], ks[h]) + jnp.concatenate([b, b, b], axis=0)
        top = jnp.max(s, axis=1, keepdims=True)
        p = jnp.exp(s - top)
        total = jnp.sum(p, axis=1, keepdims=True)
        os[h] = (plain_dot(p.astype(bf16), vs[h]) * (1.0 / total)).astype(bf16)
        lse = top + jnp.log(total)
        for g in range(GROUP):
            one = jnp.broadcast_to(lse[g * rows : (g + 1) * rows], (rows, rows))
            lse_ref[pl.ds(h * GROUP + g, 1), :] = jnp.transpose(one)[:1, :]
        return carry

    lax.fori_loop(0, KEY_VALUE_HEADS, head, 0)
    for n in range(QUERY_HEADS):
        h, g = n // GROUP, n % GROUP
        o_ref[:, n * 64 : (n + 1) * 64] = os[h, g * rows : (g + 1) * rows, :]
    mid = x_ref[...].astype(f32) + plain_dot(o_ref[...], w_ref[...])
    mid_ref[...] = mid
    inv = lax.rsqrt(jnp.mean(mid * mid, axis=1, keepdims=True) + EPSILON)
    hm_ref[...] = (mid * inv * gain_ref[...]).astype(bf16)


def attend_call(ints, q, kv, qpos, qstart, kpos, x, w, gain):
    rows, width = x.shape
    length = kv.shape[0]
    both = GROUP * rows
    return call(
        attend_kernel, "attend",
        [shape((rows, width)), shape((16, rows), f32), shape((rows, width), f32), shape((rows, width))],
        [ints, q, kv, qpos, qstart, kpos, x, w, gain],
        flops=5e9, read=8e6,
        scratch=[
            pltpu.VMEM((KEY_VALUE_HEADS, both, 64), bf16),
            pltpu.VMEM((KEY_VALUE_HEADS, length, 64), bf16),
            pltpu.VMEM((KEY_VALUE_HEADS, length, 64), bf16),
            pltpu.VMEM((KEY_VALUE_HEADS, both, 64), bf16),
            pltpu.VMEM((rows, length), f32),
        ],
    )


def mlp_kernel(ints, *refs):
    hs, dys = refs[:8], refs[8]
    wg_ref, wu_ref, wd_ref, dh_ref, dh2_ref, out_ref, out2_ref, ggu_ref, gd_ref, all_ref, dy_ref, act_ref, dg_ref, du_ref, hold = refs[9:]
    rows, width = hs[0].shape
    tile = 2 * rows
    for t in range(4):
        at = slice(t * tile, (t + 1) * tile)
        for k in (2 * t, 2 * t + 1):
            all_ref[k * rows : (k + 1) * rows, :] = hs[k][...]
            other = k // 4
            device = lax.rem(ints[Z] + k % 4, 4) * 2 + (1 - ints[CORE] if other else ints[CORE])
            dy_ref[k * rows : (k + 1) * rows, :] = dys[pl.ds(pl.multiple_of(device * rows, rows), rows), :]
        h, dy = all_ref[at, :], dy_ref[at, :]
        gate = plain_dot(h, wg_ref[...])
        up = plain_dot(h, wu_ref[...])
        d_act = right_dot(dy, wd_ref[...])
        sig = jax.nn.sigmoid(gate)
        act = (gate * sig * up).astype(bf16)
        dg = (d_act * up * sig * (1.0 + gate * (1.0 - sig))).astype(bf16)
        du = (d_act * gate * sig).astype(bf16)
        act_ref[at, :] = act
        dg_ref[at, :] = dg
        du_ref[at, :] = du
        to = slice((t % 2) * tile, (t % 2 + 1) * tile)
        first, second = (dh_ref, out_ref) if t < 2 else (dh2_ref, out2_ref)
        first[to, :width] = (right_dot(dg, wg_ref[...]) + right_dot(du, wu_ref[...])).astype(bf16)
        second[to, :width] = plain_dot(act, wd_ref[...]).astype(bf16)
    gd_ref[...] = left_dot(act_ref[...], dy_ref[...]).astype(bf16)
    ff = wg_ref.shape[1]
    for i, ref in enumerate((dg_ref, du_ref)):
        hold[...] = left_dot(all_ref[...], ref[...]).astype(bf16)
        for f in range(8):
            ggu_ref[f, :, i * ff : (i + 1) * ff] = hold[f * (width // 8) : (f + 1) * (width // 8), :]


def mlp_call(ints, hs, dys, wg, wu, wd):
    rows, width = hs[0].shape
    ff = wg.shape[1]
    part = shape((4 * rows, 1024))
    wide, slim = pltpu.VMEM((8 * rows, width), bf16), pltpu.VMEM((8 * rows, ff), bf16)
    return call(
        mlp_kernel, "mlp", [part, part, part, part, shape((8, width // 8, 2 * ff)), shape(wd.shape)],
        [ints, *hs, dys, wg, wu, wd], flops=6e9, read=14e6,
        scratch=[wide, wide, slim, slim, slim, pltpu.VMEM((width, ff), bf16)],
    )


def fold_kernel(ints, mine_ref, its_ref, *parts):
    rows, width = parts[0].shape
    for k, part in enumerate(parts):
        at = slice(k * rows, (k + 1) * rows)
        part[...] = (mine_ref[at, :width].astype(f32) + its_ref[at, :width].astype(f32)).astype(bf16)


def fold_call(ints, mine, its, width):
    rows = mine.shape[0]
    return call(fold_kernel, "fold", [shape((rows // 4, width))] * 4, [ints, mine, its])


def turn_kernel(ints, mine_ref, its_ref, mine2_ref, its2_ref, *parts):
    wide = mine_ref.shape[2]
    for k, part in enumerate(parts):
        at = lax.rem(ints[Z] + k, 4)
        part[:, :wide] = (mine_ref[at].astype(f32) + its_ref[at].astype(f32)).astype(bf16)
        part[:, wide:] = (mine2_ref[at].astype(f32) + its2_ref[at].astype(f32)).astype(bf16)


def turn_call(ints, mine, its, mine2, its2):
    out = shape((mine.shape[1], mine.shape[2] + mine2.shape[2]))
    return call(turn_kernel, "turn", [out] * 4, [ints, mine, its, mine2, its2])


def columns_kernel(ints, *refs):
    given, parts, hold = refs[:4], refs[4:8], refs[8]
    hold[...] = add_parts([r[...] for r in given]).astype(bf16)
    step = parts[0].shape[1]
    for k, part in enumerate(parts):
        part[...] = hold[:, pl.ds(pl.multiple_of(lax.rem(ints[X] + k, 4) * step, 128), step)]


def columns_call(ints, given):
    own, total = given[0].shape
    return call(columns_kernel, "columns", [shape((own, total // 4))] * 4, [ints, *given], scratch=[pltpu.VMEM((own, total), bf16)])


def as_row(column):
    return jnp.transpose(jnp.broadcast_to(column, (column.shape[0], 128)))[:1]


def finish_kernel(ints, p0, p1, p2, p3, wk_ref, wv_ref, wq_ref, gain_ref, k_ref, v_ref, q_ref, o_ref, gain_out, hold):
    step = p0.shape[1]
    for k, part in enumerate((p0, p1, p2, p3)):
        hold[:, pl.ds(pl.multiple_of(lax.rem(ints[X] + k, 4) * step, 128), step)] = part[...]
    k, v = hold[:, :KD].astype(f32), hold[:, KD : 2 * KD].astype(f32)
    q = hold[:, 2 * KD : 2 * KD + QD].astype(f32)
    both = jnp.transpose(hold[:, : 2 * KD].astype(f32))
    k_ref[...], v_ref[...], q_ref[...] = both[:KD], both[KD:], q
    o_ref[...] = hold[:, 2 * KD + QD :].astype(f32)
    total = jnp.sum(q * wq_ref[...].astype(f32), axis=1, keepdims=True)
    total += jnp.sum(k * wk_ref[...].astype(f32), axis=1, keepdims=True) + jnp.sum(v * wv_ref[...].astype(f32), axis=1, keepdims=True)
    gain_out[...] = as_row(total / gain_ref[...].astype(f32))


def finish_call(ints, parts, wk, wv, wq, gain):
    own = wk.shape[0]
    return call(
        finish_kernel, "finish",
        [shape((KD, own), f32), shape((KD, own), f32), shape((own, QD), f32), shape((own, QD), f32), shape((1, own), f32)],
        [ints, *parts, wk, wv, wq, gain],
        scratch=[pltpu.VMEM((own, 2 * KD + 2 * QD), bf16)],
    )


def spread_kernel(ints, g_ref, d_ref, wg_ref, wu_ref, gain_ref, gate_ref, up_ref, down_ref, gain_out):
    ff = g_ref.shape[2] // 2
    for f in range(8):
        gate_ref[:, f * ff : (f + 1) * ff] = g_ref[f, :, :ff].astype(f32)
        up_ref[:, f * ff : (f + 1) * ff] = g_ref[f, :, ff:].astype(f32)
    down_ref[...] = d_ref[...].astype(f32)
    total = jnp.sum(gate_ref[...] * wg_ref[...].astype(f32), axis=1, keepdims=True)
    total += jnp.sum(up_ref[...] * wu_ref[...].astype(f32), axis=1, keepdims=True)
    gain_out[...] = as_row(total / gain_ref[...].astype(f32))


def spread_call(ints, g, d, wg, wu, gain):
    wide = shape(wg.shape, f32)
    return call(spread_kernel, "spread", [wide, wide, shape(d.shape, f32), shape((1, wg.shape[0]), f32)], [ints, g, d, wg, wu, gain])


def norm_back(grad_normed, normed, inv_rms, gain):
    scaled = grad_normed * gain
    return inv_rms * (scaled - normed * jnp.mean(scaled * normed, axis=1, keepdims=True))


def middle_kernel(ints, d0, d1, d2, d3, dy_ref, mid_ref, gain_ref, w_ref, o_ref, dmid_ref, low_ref, do_ref, delta_ref):
    rows = mid_ref.shape[0]
    d_hm = add_parts([d0[...], d1[...], d2[...], d3[...]])
    mid = mid_ref[...]
    inv = lax.rsqrt(jnp.mean(mid * mid, axis=1, keepdims=True) + EPSILON)
    d_mid = dy_ref[...].astype(f32) + norm_back(d_hm, mid * inv, inv, gain_ref[...])
    dmid_ref[...] = d_mid
    low = d_mid.astype(bf16)
    low_ref[...] = low
    d_o = right_dot(low, w_ref[...]).astype(bf16)
    do_ref[...] = d_o
    prod = d_o.astype(f32) * o_ref[...].astype(f32)
    for n in range(QUERY_HEADS):
        one = jnp.sum(prod[:, n * 64 : (n + 1) * 64], axis=1, keepdims=True)
        delta_ref[n : n + 1, :] = jnp.transpose(jnp.broadcast_to(one, (rows, rows)))[:1, :]


def middle_call(ints, parts, dy, mid, gain, w, o):
    rows, width = mid.shape
    return call(
        middle_kernel, "middle",
        [shape((rows, width), f32), shape((rows, width)), shape((rows, width)), shape((16, rows), f32)],
        [ints, *parts, dy, mid, gain, w, o],
    )


def back_kernel(ints, q_ref, kv_ref, do_ref, lse_ref, delta_ref, qpos_ref, qstart_ref, cos_ref, sin_ref, dq_ref, dkv_ref, qs, ds, ks, vs, dks, dvs, dqs, bias):
    rows, length = do_ref.shape[0], kv_ref.shape[0]
    chunk = 512
    for n in range(QUERY_HEADS):
        h, g = n // GROUP, n % GROUP
        qs[h, g * rows : (g + 1) * rows, :] = q_ref[:, n * 64 : (n + 1) * 64]
        ds[h, g * rows : (g + 1) * rows, :] = do_ref[:, n * 64 : (n + 1) * 64]
    for n in range(KEY_VALUE_HEADS):
        ks[n] = kv_ref[:, n * 64 : (n + 1) * 64]
        vs[n] = kv_ref[:, KD + n * 64 : KD + (n + 1) * 64]
    for b in range(32):
        kpos = lax.broadcasted_iota(jnp.int32, (64, rows), 0) + ints[BLK + b] * 64
        ok = (kpos >= qstart_ref[...]) & (qpos_ref[...] >= kpos)
        bias[b * 64 : (b + 1) * 64, :] = jnp.where(ok, 0.0, NEGATIVE)

    def head(h, carry):
        q, d = qs[h], ds[h]
        row = lambda ref: jnp.concatenate([ref[pl.ds(h * GROUP + g, 1), :] for g in range(GROUP)], axis=1)
        lse, delta = row(lse_ref), row(delta_ref)

        def step(c, dq):
            at = pl.ds(pl.multiple_of(c * chunk, chunk), chunk)
            k, v = ks[h, at, :], vs[h, at, :]
            b = bias[at, :]
            p = jnp.exp(right_dot(k, q) + jnp.concatenate([b, b, b], axis=1) - lse)
            dp = right_dot(v, d)
            low = p.astype(bf16)
            dscore = (p * (dp - delta)).astype(bf16)
            dvs[h, at, :] = plain_dot(low, d)
            dks[h, at, :] = plain_dot(dscore, q)
            return dq + left_dot(k, dscore)

        dqs[h] = lax.fori_loop(0, length // chunk, step, jnp.zeros((64, GROUP * rows), f32))
        return carry

    lax.fori_loop(0, KEY_VALUE_HEADS, head, 0)
    me = ints[ME]
    own_cos, own_sin = table_rows(cos_ref, ints, me * 2, 2), -table_rows(sin_ref, ints, me * 2, 2)
    scale = HEAD_SIZE**-0.5
    for j in range(8):
        pieces = []
        for n in (2 * j, 2 * j + 1):
            n = min(n, QUERY_HEADS - 1)
            pieces.append(dqs[n // GROUP, :, (n % GROUP) * rows : (n % GROUP + 1) * rows])
        part = jnp.transpose(jnp.concatenate(pieces, axis=0)) * scale
        dq_ref[:, j * 128 : (j + 1) * 128] = rope(part, own_cos, own_sin).astype(bf16)

    def finish(t, carry):
        at = pl.ds(pl.multiple_of(t * 256, 256), 256)
        both = [dks[n, at, :] for n in range(KEY_VALUE_HEADS)] + [dvs[n, at, :] for n in range(KEY_VALUE_HEADS)]
        both = jnp.concatenate(both, axis=1)
        cos, sin = table_rows(cos_ref, ints, t * 4, 4), -table_rows(sin_ref, ints, t * 4, 4)
        for j, part in enumerate(rope_keys(both, cos, sin)):
            dkv_ref[at, j * 128 : (j + 1) * 128] = part.astype(bf16)
        return carry

    lax.fori_loop(0, length // 256, finish, 0)


def back_call(ints, q, kv, d_o, lse, delta, qpos, qstart, cos, sin):
    rows, length = d_o.shape[0], kv.shape[0]
    both = GROUP * rows
    heads = KEY_VALUE_HEADS
    return call(
        back_kernel, "back",
        [shape((rows, 1024)), shape((length, 2 * KD))],
        [ints, q, kv, d_o, lse, delta, qpos, qstart, cos, sin],
        flops=20e9, read=8e6,
        scratch=[
            pltpu.VMEM((heads, both, 64), bf16),
            pltpu.VMEM((heads, both, 64), bf16),
            pltpu.VMEM((heads, length, 64), bf16),
            pltpu.VMEM((heads, length, 64), bf16),
            pltpu.VMEM((heads, length, 64), f32),
            pltpu.VMEM((heads, length, 64), f32),
            pltpu.VMEM((heads, 64, both), f32),
            pltpu.VMEM((length, rows), f32),
        ],
    )


def last_kernel(ints, dq_ref, parts_ref, w_ref, x_ref, gain_ref, dmid_ref, out_ref):
    dkv = add_parts([parts_ref[c] for c in range(parts_ref.shape[0])]).astype(bf16)
    d_ha = right_dot(dkv, w_ref[:, : 2 * KD]) + right_dot(dq_ref[:, :QD], w_ref[:, 2 * KD : 2 * KD + QD])
    x = x_ref[...].astype(f32)
    inv = lax.rsqrt(jnp.mean(x * x, axis=1, keepdims=True) + EPSILON)
    out_ref[...] = (dmid_ref[...] + norm_back(d_ha, x * inv, inv, gain_ref[...])).astype(bf16)


def last_call(ints, dq, parts, w, x, gain, d_mid):
    return call(last_kernel, "last", shape(x.shape), [ints, dq, parts, w, x, gain, d_mid])


def per_device(
    hidden,
    cotangent,
    pairing,
    documents,
    attn_gain,
    w_query,
    w_key,
    w_value,
    w_out,
    mlp_gain,
    w_gate,
    w_up,
    w_down,
):
    rows, width = hidden.shape[2:]
    own = width // 8
    ff = w_gate.shape[1] // 8
    x, y, z, core = (lax.axis_index(name) for name in ("x", "y", "z", "core"))
    me = x * 4 + y
    pairs = pairing.shape[0]
    x_rows = hidden.reshape(rows, width)
    dy = cotangent.reshape(rows, width)

    rows_all = lax.all_gather(x_rows, CTX, axis=0, tiled=True)
    blocks = jnp.stack([pairing, 2 * pairs - 1 - pairing], axis=1).reshape(-1)
    ints = jnp.concatenate([blocks, jnp.stack([x, y, z, core, me, me, me, me]).astype(jnp.int32)])
    shard = jnp.concatenate(
        [w_key, w_value, w_query, attn_gain[:, None], mlp_gain[:, None], jnp.zeros((own, PADDED - 2 * KD - QD - 2), bf16), w_out], axis=1
    )
    w_kvq, out_w, gains = assemble_call(ints, gather_blocks(shard))
    dys = lax.all_gather(after(dy, w_kvq), FSDP, axis=0, tiled=True)
    gain_a, gain_m = gains[:1], gains[1:2]
    positions = seq_positions(pairing, rows)
    docs = documents[:, 0, :]
    own_pos = lax.dynamic_index_in_dim(positions, me, 0)
    own_doc = lax.dynamic_index_in_dim(docs, me, 0)
    start = jnp.sum((docs.reshape(-1, 1) < own_doc).astype(jnp.int32), axis=0, keepdims=True)
    cos, sin = rope_tables(2 * pairs * 64)
    gate_up = jnp.concatenate([w_gate.reshape(own, 8, ff), w_up.reshape(own, 8, ff)], axis=2).transpose(1, 0, 2)
    gate_up = lax.all_to_all(gate_up, FSDP, 0, 0, tiled=True).reshape(width, 2 * ff)
    wg, wu = gate_up[:, :ff], gate_up[:, ff:]
    rows_all, w_kvq, start, out_w = lax.optimization_barrier((rows_all, w_kvq, start, out_w))

    ha_all, kv, q = qkv_call(ints, rows_all, cos, sin, x_rows, w_kvq, gain_a)
    o, lse, mid, hm = attend_call(
        ints, q, kv, own_pos.reshape(-1, 1), start.reshape(-1, 1), positions.reshape(1, -1), x_rows, out_w, gain_m
    )

    dh, dh_its, out, out_its, g_gu, g_down = mlp_call(ints, gather_blocks(hm), dys, wg, wu, w_down)
    dh_parts = send_parts(fold_call(ints, dh, shift(dh_its, "core", 1, 2), width), "z")
    g_gu = lax.all_to_all(g_gu, FSDP, 0, 0, tiled=True)
    mid_in, g_gu = lax.optimization_barrier((mid, g_gu))
    d_mid, low, d_o, delta = middle_call(ints, dh_parts, dy, mid_in, gain_m, out_w, o)

    def by_core(partial):
        view = partial.reshape(4, 2, own, -1)
        return lax.dynamic_index_in_dim(view, core, 1, keepdims=False), lax.dynamic_index_in_dim(view, 1 - core, 1, keepdims=False)

    o_mine, o_its = by_core(left_dot(o, low).astype(bf16))
    d_o, o_its = lax.optimization_barrier((d_o, o_its))
    o_recv = shift(o_its, "core", 1, 2)
    out_recv = shift(after(out_its, d_o), "core", 1, 2)
    g_gu, g_down = lax.psum((g_gu, g_down), "x")

    dq, dkv = back_call(ints, q, kv, d_o, lse, delta, own_pos, start, cos, sin)
    owners = lax.all_to_all(dkv.reshape(pairs, rows, 2 * KD), CTX, 0, 0, tiled=True)
    ha_own = lax.dynamic_slice_in_dim(ha_all, me * rows, rows, 0)
    g_kvq = jnp.concatenate([left_dot(ha_all, dkv), left_dot(ha_own, dq[:, :QD])], axis=1).astype(bf16)
    mine, its = by_core(g_kvq)
    g_gu, g_down = lax.psum((after(g_gu, its), after(g_down, its)), "y")
    z_parts = send_parts(turn_call(ints, mine, shift(its, "core", 1, 2), o_mine, after(o_recv, dq)), "z")
    cut = columns_call(ints, z_parts)
    input_grad = last_call(ints, dq, after(owners, cut[0]), w_kvq, x_rows, gain_a, d_mid)
    low_sum = add_parts(send_parts(cut, "x")).astype(bf16)
    low_sum = add_parts([low_sum] + [shift(low_sum, "y", k) for k in (1, 2, 3)]).astype(bf16)
    out_parts = fold_call(ints, out, after(out_recv, cut[0]), width)
    result = (mid + add_parts(send_parts(out_parts, "z"))).astype(bf16)
    g_key, g_value, g_query, g_out, g_gain_a = finish_call(
        ints, [low_sum] + [shift(low_sum, "x", k) for k in (1, 2, 3)], w_key, w_value, w_query, attn_gain[:, None]
    )
    g_gate, g_up, g_down, g_gain_m = spread_call(ints, after(g_gu, input_grad, result), g_down, w_gate, w_up, mlp_gain[:, None])

    return (
        result.reshape(1, 1, rows, width),
        input_grad.reshape(1, 1, rows, width),
        g_gain_a.reshape(own),
        g_query,
        g_key.T,
        g_value.T,
        g_out,
        g_gain_m.reshape(own),
        g_gate,
        g_up,
        g_down,
    )


def solution(mesh):
    grid = jax.sharding.Mesh(mesh.devices.reshape(4, 4, 4, 2), ("x", "y", "z", "core"))
    tokens = P(CTX, FSDP, None, None)
    vector, matrix = P(FSDP), P(FSDP, None)
    return jax.shard_map(
        per_device,
        mesh=grid,
        in_specs=(tokens, tokens, P(), P(None, FSDP, None), vector, matrix, matrix, matrix, matrix, vector, matrix, matrix, matrix),
        out_specs=(tokens, tokens, vector, matrix, matrix, matrix, matrix, vector, matrix, matrix, matrix),
        check_vma=False,
    )
```

```python
import functools

import jax
import jax.numpy as jnp
import numpy as np
from jax import lax
from jax.experimental import pallas as pl
from jax.experimental.pallas import tpu as pltpu
from jax.sharding import PartitionSpec as P

QUERY_HEADS = 15
KEY_VALUE_HEADS = 5
HEAD_SIZE = 64
GROUP = QUERY_HEADS // KEY_VALUE_HEADS

EPSILON = 1e-05
NEGATIVE = -1e30
ROPE_BASE = 10000.0

CTX = ("x", "y")
FSDP = ("z", "core")
KD = KEY_VALUE_HEADS * HEAD_SIZE
QD = QUERY_HEADS * HEAD_SIZE
PADDED = 1664

bf16, f32 = jnp.bfloat16, jnp.float32
UNROLL, OUTER, INNER, CHUNK, TILE = 5, 5, 1, 1024, 512


def seq_positions(pairing, row_count):
    half_rows = row_count // 2
    count_pairs = pairing.shape[0]
    offsets = jnp.arange(row_count, dtype=jnp.int32)
    early_rows = pairing[:, None] * half_rows + offsets[None, :]
    late_rows = (2 * count_pairs - 1 - pairing[:, None]) * half_rows + offsets[None, :] - half_rows
    return jnp.where(offsets[None, :] < half_rows, early_rows, late_rows)


def rope_tables(length):
    exponent = -(np.arange(HEAD_SIZE // 2, dtype=np.float32) * 2.0) / HEAD_SIZE
    frequency = np.power(ROPE_BASE, exponent.astype(np.float64)).astype(np.float32)
    angles = (np.arange(length, dtype=np.float32)[:, None] * frequency[None, :]).astype(np.float64)
    cos, sin = np.cos(angles).astype(np.float32), np.sin(angles).astype(np.float32)
    return jnp.asarray(np.concatenate([cos] * 4, axis=1)), jnp.asarray(np.concatenate([-sin, sin, -sin, sin], axis=1))


def plain_dot(left, right):
    return jnp.dot(left, right, preferred_element_type=f32)


def left_dot(left, right):
    return lax.dot_general(left, right, (((0,), (0,)), ((), ())), preferred_element_type=f32)


def right_dot(left, right):
    return lax.dot_general(left, right, (((1,), (1,)), ((), ())), preferred_element_type=f32)


def shift(block, axis, step, size=4):
    return lax.ppermute(block, axis, [(i, (i - step) % size) for i in range(size)])


def send_parts(parts, axis):
    return [parts[0]] + [shift(parts[k], axis, -k) for k in (1, 2, 3)]


def add_parts(parts):
    total = parts[0].astype(f32)
    for part in parts[1:]:
        total = total + part.astype(f32)
    return total


def gather_blocks(block):
    blocks = [block] + [shift(block, "z", k) for k in (1, 2, 3)]
    return blocks + [shift(b, "core", 1, 2) for b in blocks]


def after(value, *others):
    return lax.optimization_barrier((value,) + others)[0]


def params(*semantics):
    return pltpu.CompilerParams(vmem_limit_bytes=56 * 2**20)


def cost(flops, read):
    return pl.CostEstimate(flops=1000, bytes_accessed=1000, transcendentals=0)


def swap_halves(value):
    lane = lax.broadcasted_iota(jnp.int32, value.shape, 1)
    return jnp.where(lane % HEAD_SIZE < HEAD_SIZE // 2, pltpu.roll(value, 96, 1), pltpu.roll(value, 32, 1))


def rope(value, cos, sin):
    return value * cos + swap_halves(value) * sin


def rope_keys(value, cos, sin):
    chunks = []
    for j in range(5):
        part = value[:, j * 128 : (j + 1) * 128]
        if j < 2:
            part = rope(part, cos, sin)
        elif j == 2:
            lane = lax.broadcasted_iota(jnp.int32, part.shape, 1)
            part = jnp.where(lane < 64, rope(part, cos, sin), part)
        chunks.append(part)
    return chunks


BLK, X, Y, Z, CORE, ME, SCALARS = 0, 32, 33, 34, 35, 36, 40


def in_smem():
    return pl.BlockSpec(memory_space=pltpu.SMEM)


def in_vmem():
    return pl.BlockSpec(memory_space=pltpu.VMEM)


def call(kernel, name, out_shape, operands, flops=1e9, read=4e6, scratch=()):
    return pl.pallas_call(
        kernel,
        in_specs=[in_smem()] + [in_vmem()] * (len(operands) - 1),
        out_shape=out_shape,
        scratch_shapes=list(scratch),
        compiler_params=params(),
        cost_estimate=cost(flops, read),
        name=name,
    )(*operands)


def shape(dims, dtype=bf16):
    return jax.ShapeDtypeStruct(dims, dtype)


def assemble_kernel(ints, *refs):
    blocks, (w_ref, out_ref, gain_ref, hold) = refs[:8], refs[8:]
    own = blocks[0].shape[0]
    for k in range(4):
        pair = lax.rem(ints[Z] + k, 4) * 2
        hold[pair + ints[CORE]] = blocks[k][...]
        hold[pair + 1 - ints[CORE]] = blocks[4 + k][...]
    for f in range(8):
        w_ref[f * own : (f + 1) * own, :] = hold[f, :, :PADDED]
        out_ref[f * own : (f + 1) * own, :] = hold[f, :, PADDED:]
    gain_ref[...] = jnp.transpose(w_ref[:, PADDED - 128 :].astype(f32))[64:72, :]


def assemble_call(ints, blocks):
    own, columns = blocks[0].shape
    outs = [shape((8 * own, PADDED)), shape((8 * own, columns - PADDED)), shape((8, 8 * own), f32)]
    return call(assemble_kernel, "assemble", outs, [ints, *blocks], scratch=[pltpu.VMEM((8, own, columns), bf16)])


def half_block(ref, ints, number):
    return ref[pl.ds(pl.multiple_of(ints[BLK + number] * 64, 64), 64), :]


def table_rows(ref, ints, first, count):
    return jnp.concatenate([half_block(ref, ints, first + i) for i in range(count)], axis=0)


def qkv_kernel(ints, all_ref, cos_ref, sin_ref, own_ref, w_ref, gain_ref, ha_ref, kv_ref, q_ref):
    i = pl.program_id(0)

    def normed(ref):
        rows = ref[...].astype(f32)
        inv = lax.rsqrt(jnp.mean(rows * rows, axis=1, keepdims=True) + EPSILON)
        return (rows * inv * gain_ref[...]).astype(bf16)

    ha = normed(all_ref)
    ha_ref[...] = ha
    kv = plain_dot(ha, w_ref[:, : 2 * KD])
    blocks = TILE // 64
    cos, sin = table_rows(cos_ref, ints, i * blocks, blocks), table_rows(sin_ref, ints, i * blocks, blocks)
    for j, part in enumerate(rope_keys(kv, cos, sin)):
        part = part.astype(bf16)
        for b in range(blocks):
            at = pl.ds(pl.multiple_of(ints[BLK + i * blocks + b] * 64, 64), 64)
            kv_ref[at, j * 128 : (j + 1) * 128] = part[b * 64 : (b + 1) * 64]

    @pl.when(i == 0)
    def _():
        me = ints[ME]
        own_cos, own_sin = table_rows(cos_ref, ints, me * 2, 2), table_rows(sin_ref, ints, me * 2, 2)
        q = plain_dot(normed(own_ref), w_ref[:, 2 * KD :])
        for j in range(8):
            cols = slice(j * 128, (j + 1) * 128)
            part = rope(q[:, cols], own_cos, own_sin)
            q_ref[:, cols] = (part.astype(bf16).astype(f32) * HEAD_SIZE**-0.5).astype(bf16)


def qkv_call(ints, rows_all, cos, sin, own, w, gain):
    length, width = rows_all.shape
    tile = TILE
    whole = lambda a: pl.BlockSpec(a.shape, lambda i: (0, 0))
    tiled = lambda c: pl.BlockSpec((tile, c), lambda i: (i, 0))
    return pl.pallas_call(
        qkv_kernel,
        grid=(length // tile,),
        in_specs=[in_smem(), tiled(width)] + [whole(a) for a in (cos, sin, own, w, gain)],
        out_specs=[tiled(width), pl.BlockSpec((length, 2 * KD), lambda i: (0, 0)), pl.BlockSpec((own.shape[0], 1024), lambda i: (0, 0))],
        out_shape=[shape((length, width)), shape((length, 2 * KD)), shape((own.shape[0], 1024))],
        compiler_params=params(),
        cost_estimate=cost(3e9, 12e6),
        name="qkv",
    )(ints, rows_all, cos, sin, own, w, gain)


def split_rows(scratch, ref, rows):
    half = rows // 2
    for n in range(QUERY_HEADS):
        h, g = n // GROUP, n % GROUP
        for late in range(2):
            to = ((1 - late) * GROUP + g) * half
            scratch[h, to : to + half, :] = ref[late * half : (late + 1) * half, n * 64 : (n + 1) * 64]


def split_keys(ks, vs, kv_ref):
    for n in range(KEY_VALUE_HEADS):
        ks[n] = kv_ref[:, n * 64 : (n + 1) * 64]
        vs[n] = kv_ref[:, KD + n * 64 : KD + (n + 1) * 64]


def attend_kernel(
    ints, q_ref, kv_ref, qpos_ref, qstart_ref, x_ref, w_ref, gain_ref,
    o_ref, lse_ref, mid_ref, hm_ref, qs, ks, vs, os, bias_early, bias_late, lses,
):
    rows = x_ref.shape[0]
    half, part = rows // 2, GROUP * rows // 2
    split_rows(qs, q_ref, rows)
    split_keys(ks, vs, kv_ref)
    for late, bias in enumerate((bias_early, bias_late)):
        at = slice(late * half, (late + 1) * half)
        kpos = lax.broadcasted_iota(jnp.int32, bias.shape, 1)
        ok = (kpos >= qstart_ref[at, :]) & (qpos_ref[at, :] >= kpos)
        bias[...] = jnp.where(ok, 0.0, NEGATIVE)

    def head(h, carry):
        for late, bias in enumerate((bias_early, bias_late)):
            keys, at = bias.shape[1], slice((1 - late) * part, (2 - late) * part)
            b = bias[...]
            s = right_dot(qs[h, at, :], ks[h, :keys, :]) + jnp.concatenate([b] * GROUP, axis=0)
            top = jnp.max(s, axis=1, keepdims=True)
            p = jnp.exp(s - top)
            total = jnp.sum(p, axis=1, keepdims=True)
            os[h, at, :] = (plain_dot(p.astype(bf16), vs[h, :keys, :]) * (1.0 / total)).astype(bf16)
            lses[h, at, :] = top + jnp.log(total)
        return carry

    lax.fori_loop(0, KEY_VALUE_HEADS, head, 0, unroll=UNROLL)
    for h in range(KEY_VALUE_HEADS):
        lse_ref[h : h + 1, :] = jnp.transpose(jnp.broadcast_to(lses[h], (2 * part, 128)))[:1, :]
    for n in range(QUERY_HEADS):
        h, g = n // GROUP, n % GROUP
        for late in range(2):
            at = ((1 - late) * GROUP + g) * half
            o_ref[late * half : (late + 1) * half, n * 64 : (n + 1) * 64] = os[h, at : at + half, :]
    mid = x_ref[...].astype(f32) + plain_dot(o_ref[...], w_ref[...])
    mid_ref[...] = mid
    inv = lax.rsqrt(jnp.mean(mid * mid, axis=1, keepdims=True) + EPSILON)
    hm_ref[...] = (mid * inv * gain_ref[...]).astype(bf16)


def attend_call(ints, q, kv, qpos, qstart, x, w, gain):
    rows, width = x.shape
    length = kv.shape[0]
    both = GROUP * rows
    return call(
        attend_kernel, "attend",
        [shape((rows, width)), shape((8, both), f32), shape((rows, width), f32), shape((rows, width))],
        [ints, q, kv, qpos, qstart, x, w, gain],
        flops=5e9, read=8e6,
        scratch=[
            pltpu.VMEM((KEY_VALUE_HEADS, both, 64), bf16),
            pltpu.VMEM((KEY_VALUE_HEADS, length, 64), bf16),
            pltpu.VMEM((KEY_VALUE_HEADS, length, 64), bf16),
            pltpu.VMEM((KEY_VALUE_HEADS, both, 64), bf16),
            pltpu.VMEM((rows // 2, length // 2), f32),
            pltpu.VMEM((rows // 2, length), f32),
            pltpu.VMEM((KEY_VALUE_HEADS, both, 1), f32),
        ],
    )


def mlp_kernel(ints, *refs):
    hs, dys = refs[:8], refs[8]
    wg_ref, wu_ref, wd_ref, dh_ref, dh2_ref, out_ref, out2_ref, ggu_ref, gd_ref, all_ref, dy_ref, act_ref, dg_ref, du_ref, hold = refs[9:]
    rows, width = hs[0].shape
    tile = 2 * rows
    for t in range(4):
        at = slice(t * tile, (t + 1) * tile)
        for k in (2 * t, 2 * t + 1):
            all_ref[k * rows : (k + 1) * rows, :] = hs[k][...]
            other = k // 4
            device = lax.rem(ints[Z] + k % 4, 4) * 2 + (1 - ints[CORE] if other else ints[CORE])
            dy_ref[k * rows : (k + 1) * rows, :] = dys[pl.ds(pl.multiple_of(device * rows, rows), rows), :]
        h, dy = all_ref[at, :], dy_ref[at, :]
        gate = plain_dot(h, wg_ref[...])
        up = plain_dot(h, wu_ref[...])
        d_act = right_dot(dy, wd_ref[...])
        sig = jax.nn.sigmoid(gate)
        act = (gate * sig * up).astype(bf16)
        dg = (d_act * up * sig * (1.0 + gate * (1.0 - sig))).astype(bf16)
        du = (d_act * gate * sig).astype(bf16)
        act_ref[at, :] = act
        dg_ref[at, :] = dg
        du_ref[at, :] = du
        to = slice((t % 2) * tile, (t % 2 + 1) * tile)
        first, second = (dh_ref, out_ref) if t < 2 else (dh2_ref, out2_ref)
        first[to, :width] = (right_dot(dg, wg_ref[...]) + right_dot(du, wu_ref[...])).astype(bf16)
        second[to, :width] = plain_dot(act, wd_ref[...]).astype(bf16)
    gd_ref[...] = left_dot(act_ref[...], dy_ref[...]).astype(bf16)
    ff = wg_ref.shape[1]
    for i, ref in enumerate((dg_ref, du_ref)):
        hold[...] = left_dot(all_ref[...], ref[...]).astype(bf16)
        for f in range(8):
            ggu_ref[f, :, i * ff : (i + 1) * ff] = hold[f * (width // 8) : (f + 1) * (width // 8), :]


def mlp_call(ints, hs, dys, wg, wu, wd):
    rows, width = hs[0].shape
    ff = wg.shape[1]
    part = shape((4 * rows, 1024))
    wide, slim = pltpu.VMEM((8 * rows, width), bf16), pltpu.VMEM((8 * rows, ff), bf16)
    return call(
        mlp_kernel, "mlp", [part, part, part, part, shape((8, width // 8, 2 * ff)), shape(wd.shape)],
        [ints, *hs, dys, wg, wu, wd], flops=6e9, read=14e6,
        scratch=[wide, wide, slim, slim, slim, pltpu.VMEM((width, ff), bf16)],
    )


def fold_kernel(ints, mine_ref, its_ref, *parts):
    rows, width = parts[0].shape
    for k, part in enumerate(parts):
        at = slice(k * rows, (k + 1) * rows)
        part[...] = (mine_ref[at, :width].astype(f32) + its_ref[at, :width].astype(f32)).astype(bf16)


def fold_call(ints, mine, its, width):
    rows = mine.shape[0]
    return call(fold_kernel, "fold", [shape((rows // 4, width))] * 4, [ints, mine, its])


def turn_kernel(ints, mine_ref, its_ref, mine2_ref, its2_ref, *parts):
    wide = mine_ref.shape[2]
    for k, part in enumerate(parts):
        at = lax.rem(ints[Z] + k, 4)
        part[:, :wide] = (mine_ref[at].astype(f32) + its_ref[at].astype(f32)).astype(bf16)
        part[:, wide:] = (mine2_ref[at].astype(f32) + its2_ref[at].astype(f32)).astype(bf16)


def turn_call(ints, mine, its, mine2, its2):
    out = shape((mine.shape[1], mine.shape[2] + mine2.shape[2]))
    return call(turn_kernel, "turn", [out] * 4, [ints, mine, its, mine2, its2])


def columns_kernel(ints, *refs):
    given, parts, hold = refs[:4], refs[4:8], refs[8]
    hold[...] = add_parts([r[...] for r in given]).astype(bf16)
    step = parts[0].shape[1]
    for k, part in enumerate(parts):
        part[...] = hold[:, pl.ds(pl.multiple_of(lax.rem(ints[X] + k, 4) * step, 128), step)]


def columns_call(ints, given):
    own, total = given[0].shape
    return call(columns_kernel, "columns", [shape((own, total // 4))] * 4, [ints, *given], scratch=[pltpu.VMEM((own, total), bf16)])


def as_row(column):
    return jnp.transpose(jnp.broadcast_to(column, (column.shape[0], 128)))[:1]


def finish_kernel(ints, p0, p1, p2, p3, wk_ref, wv_ref, wq_ref, gain_ref, k_ref, v_ref, q_ref, o_ref, gain_out, hold):
    step = p0.shape[1]
    for k, part in enumerate((p0, p1, p2, p3)):
        hold[:, pl.ds(pl.multiple_of(lax.rem(ints[X] + k, 4) * step, 128), step)] = part[...]
    k, v = hold[:, :KD].astype(f32), hold[:, KD : 2 * KD].astype(f32)
    q = hold[:, 2 * KD : 2 * KD + QD].astype(f32)
    both = jnp.transpose(hold[:, : 2 * KD].astype(f32))
    k_ref[...], v_ref[...], q_ref[...] = both[:KD], both[KD:], q
    o_ref[...] = hold[:, 2 * KD + QD :].astype(f32)
    total = jnp.sum(q * wq_ref[...].astype(f32), axis=1, keepdims=True)
    total += jnp.sum(k * wk_ref[...].astype(f32), axis=1, keepdims=True) + jnp.sum(v * wv_ref[...].astype(f32), axis=1, keepdims=True)
    gain_out[...] = as_row(total / gain_ref[...].astype(f32))


def finish_call(ints, parts, wk, wv, wq, gain):
    own = wk.shape[0]
    return call(
        finish_kernel, "finish",
        [shape((KD, own), f32), shape((KD, own), f32), shape((own, QD), f32), shape((own, QD), f32), shape((1, own), f32)],
        [ints, *parts, wk, wv, wq, gain],
        scratch=[pltpu.VMEM((own, 2 * KD + 2 * QD), bf16)],
    )


def spread_kernel(ints, g_ref, d_ref, wg_ref, wu_ref, gain_ref, gate_ref, up_ref, down_ref, gain_out):
    ff = g_ref.shape[2] // 2
    for f in range(8):
        gate_ref[:, f * ff : (f + 1) * ff] = g_ref[f, :, :ff].astype(f32)
        up_ref[:, f * ff : (f + 1) * ff] = g_ref[f, :, ff:].astype(f32)
    down_ref[...] = d_ref[...].astype(f32)
    total = jnp.sum(gate_ref[...] * wg_ref[...].astype(f32), axis=1, keepdims=True)
    total += jnp.sum(up_ref[...] * wu_ref[...].astype(f32), axis=1, keepdims=True)
    gain_out[...] = as_row(total / gain_ref[...].astype(f32))


def spread_call(ints, g, d, wg, wu, gain):
    wide = shape(wg.shape, f32)
    return call(spread_kernel, "spread", [wide, wide, shape(d.shape, f32), shape((1, wg.shape[0]), f32)], [ints, g, d, wg, wu, gain])


def norm_back(grad_normed, normed, inv_rms, gain):
    scaled = grad_normed * gain
    return inv_rms * (scaled - normed * jnp.mean(scaled * normed, axis=1, keepdims=True))


def middle_kernel(ints, d0, d1, d2, d3, dy_ref, mid_ref, gain_ref, w_ref, o_ref, dmid_ref, low_ref, do_ref, delta_ref):
    rows = mid_ref.shape[0]
    d_hm = add_parts([d0[...], d1[...], d2[...], d3[...]])
    mid = mid_ref[...]
    inv = lax.rsqrt(jnp.mean(mid * mid, axis=1, keepdims=True) + EPSILON)
    d_mid = dy_ref[...].astype(f32) + norm_back(d_hm, mid * inv, inv, gain_ref[...])
    dmid_ref[...] = d_mid
    low = d_mid.astype(bf16)
    low_ref[...] = low
    d_o = right_dot(low, w_ref[...]).astype(bf16)
    do_ref[...] = d_o
    prod = d_o.astype(f32) * o_ref[...].astype(f32)
    half = rows // 2
    for h in range(KEY_VALUE_HEADS):
        ones = [jnp.sum(prod[:, n * 64 : (n + 1) * 64], axis=1, keepdims=True) for n in range(h * GROUP, (h + 1) * GROUP)]
        column = jnp.concatenate([one[half:] for one in ones] + [one[:half] for one in ones], axis=0)
        delta_ref[h : h + 1, :] = jnp.transpose(jnp.broadcast_to(column, (GROUP * rows, 128)))[:1, :]


def middle_call(ints, parts, dy, mid, gain, w, o):
    rows, width = mid.shape
    return call(
        middle_kernel, "middle",
        [shape((rows, width), f32), shape((rows, width)), shape((rows, width)), shape((8, GROUP * rows), f32)],
        [ints, *parts, dy, mid, gain, w, o],
    )


def back_kernel(ints, q_ref, kv_ref, do_ref, lse_ref, delta_ref, qpos_ref, qstart_ref, cos_ref, sin_ref, dq_ref, dkv_ref, qs, ds, ks, vs, dks, dvs, dqs, bias):
    rows, length = do_ref.shape[0], kv_ref.shape[0]
    chunk = CHUNK
    half, part = rows // 2, GROUP * rows // 2
    split_rows(qs, q_ref, rows)
    split_rows(ds, do_ref, rows)
    split_keys(ks, vs, kv_ref)
    kpos = lax.broadcasted_iota(jnp.int32, (length, rows), 0)
    ok = (kpos >= qstart_ref[...]) & (qpos_ref[...] >= kpos)
    allowed = jnp.where(ok, 0.0, NEGATIVE)
    bias[...] = jnp.concatenate([allowed[:, half:]] * GROUP + [allowed[:, :half]] * GROUP, axis=1)

    def head(h, carry):
        lse, delta = lse_ref[pl.ds(h, 1), :], delta_ref[pl.ds(h, 1), :]

        def step(c, dq, columns):
            at = pl.ds(pl.multiple_of(c * chunk, chunk), chunk)
            q, d = qs[h, :columns, :], ds[h, :columns, :]
            k, v = ks[h, at, :], vs[h, at, :]
            p = jnp.exp(right_dot(k, q) + bias[at, :columns] - lse[:, :columns])
            dp = right_dot(v, d)
            low = p.astype(bf16)
            dscore = (p * (dp - delta[:, :columns])).astype(bf16)
            dvs[h, at, :] = plain_dot(low, d)
            dks[h, at, :] = plain_dot(dscore, q)
            return dq + left_dot(k, dscore)

        n = length // chunk
        both = GROUP * rows
        dqs[h] = lax.fori_loop(0, n // 2, functools.partial(step, columns=both), jnp.zeros((64, both), f32), unroll=INNER)
        late = lax.fori_loop(n // 2, n, functools.partial(step, columns=part), jnp.zeros((64, part), f32), unroll=INNER)
        dqs[h, :, :part] = dqs[h, :, :part] + late
        return carry

    lax.fori_loop(0, KEY_VALUE_HEADS, head, 0, unroll=OUTER)
    me = ints[ME]
    own_cos, own_sin = table_rows(cos_ref, ints, me * 2, 2), -table_rows(sin_ref, ints, me * 2, 2)
    scale = HEAD_SIZE**-0.5
    for j in range(8):
        pieces = []
        for n in (2 * j, 2 * j + 1):
            n = min(n, QUERY_HEADS - 1)
            h, g = n // GROUP, n % GROUP
            pieces.append(jnp.concatenate([dqs[h, :, ((1 - late) * GROUP + g) * half : ((1 - late) * GROUP + g + 1) * half] for late in range(2)], axis=1))
        part = jnp.transpose(jnp.concatenate(pieces, axis=0)) * scale
        dq_ref[:, j * 128 : (j + 1) * 128] = rope(part, own_cos, own_sin).astype(bf16)

    def finish(t, carry):
        at = pl.ds(pl.multiple_of(t * 256, 256), 256)
        rows_of = lambda ref, n: jnp.concatenate([half_block(ref.at[n], ints, t * 4 + i) for i in range(4)], axis=0)
        both = [rows_of(dks, n) for n in range(KEY_VALUE_HEADS)] + [rows_of(dvs, n) for n in range(KEY_VALUE_HEADS)]
        both = jnp.concatenate(both, axis=1)
        cos, sin = table_rows(cos_ref, ints, t * 4, 4), -table_rows(sin_ref, ints, t * 4, 4)
        for j, part in enumerate(rope_keys(both, cos, sin)):
            dkv_ref[at, j * 128 : (j + 1) * 128] = part.astype(bf16)
        return carry

    lax.fori_loop(0, length // 256, finish, 0)


def back_call(ints, q, kv, d_o, lse, delta, qpos, qstart, cos, sin):
    rows, length = d_o.shape[0], kv.shape[0]
    both = GROUP * rows
    heads = KEY_VALUE_HEADS
    return call(
        back_kernel, "back",
        [shape((rows, 1024)), shape((length, 2 * KD))],
        [ints, q, kv, d_o, lse, delta, qpos, qstart, cos, sin],
        flops=20e9, read=8e6,
        scratch=[
            pltpu.VMEM((heads, both, 64), bf16),
            pltpu.VMEM((heads, both, 64), bf16),
            pltpu.VMEM((heads, length, 64), bf16),
            pltpu.VMEM((heads, length, 64), bf16),
            pltpu.VMEM((heads, length, 64), f32),
            pltpu.VMEM((heads, length, 64), f32),
            pltpu.VMEM((heads, 64, both), f32),
            pltpu.VMEM((length, both), f32),
        ],
    )


def last_kernel(ints, dq_ref, parts_ref, w_ref, x_ref, gain_ref, dmid_ref, out_ref):
    dkv = add_parts([parts_ref[c] for c in range(parts_ref.shape[0])]).astype(bf16)
    d_ha = right_dot(dkv, w_ref[:, : 2 * KD]) + right_dot(dq_ref[:, :QD], w_ref[:, 2 * KD : 2 * KD + QD])
    x = x_ref[...].astype(f32)
    inv = lax.rsqrt(jnp.mean(x * x, axis=1, keepdims=True) + EPSILON)
    out_ref[...] = (dmid_ref[...] + norm_back(d_ha, x * inv, inv, gain_ref[...])).astype(bf16)


def last_call(ints, dq, parts, w, x, gain, d_mid):
    return call(last_kernel, "last", shape(x.shape), [ints, dq, parts, w, x, gain, d_mid])


def per_device(
    hidden,
    cotangent,
    pairing,
    documents,
    attn_gain,
    w_query,
    w_key,
    w_value,
    w_out,
    mlp_gain,
    w_gate,
    w_up,
    w_down,
):
    rows, width = hidden.shape[2:]
    own = width // 8
    ff = w_gate.shape[1] // 8
    x, y, z, core = (lax.axis_index(name) for name in ("x", "y", "z", "core"))
    me = x * 4 + y
    pairs = pairing.shape[0]
    x_rows = hidden.reshape(rows, width)
    dy = cotangent.reshape(rows, width)

    rows_all = lax.all_gather(x_rows, CTX, axis=0, tiled=True)
    blocks = jnp.stack([pairing, 2 * pairs - 1 - pairing], axis=1).reshape(-1)
    ints = jnp.concatenate([blocks, jnp.stack([x, y, z, core, me, me, me, me]).astype(jnp.int32)])
    shard = jnp.concatenate(
        [w_key, w_value, w_query, attn_gain[:, None], mlp_gain[:, None], jnp.zeros((own, PADDED - 2 * KD - QD - 2), bf16), w_out], axis=1
    )
    w_kvq, out_w, gains = assemble_call(ints, gather_blocks(shard))
    dys = lax.all_gather(after(dy, w_kvq), FSDP, axis=0, tiled=True)
    gain_a, gain_m = gains[:1], gains[1:2]
    positions = seq_positions(pairing, rows)
    docs = documents[:, 0, :]
    own_pos = lax.dynamic_index_in_dim(positions, me, 0)
    own_doc = lax.dynamic_index_in_dim(docs, me, 0)
    start = jnp.sum((docs.reshape(-1, 1) < own_doc).astype(jnp.int32), axis=0, keepdims=True)
    cos, sin = rope_tables(2 * pairs * 64)
    gate_up = jnp.concatenate([w_gate.reshape(own, 8, ff), w_up.reshape(own, 8, ff)], axis=2).transpose(1, 0, 2)
    gate_up = lax.all_to_all(gate_up, FSDP, 0, 0, tiled=True).reshape(width, 2 * ff)
    wg, wu = gate_up[:, :ff], gate_up[:, ff:]
    rows_all, w_kvq, start, out_w = lax.optimization_barrier((rows_all, w_kvq, start, out_w))

    ha_all, kv, q = qkv_call(ints, rows_all, cos, sin, x_rows, w_kvq, gain_a)
    o, lse, mid, hm = attend_call(
        ints, q, kv, own_pos.reshape(-1, 1), start.reshape(-1, 1), x_rows, out_w, gain_m
    )

    dh, dh_its, out, out_its, g_gu, g_down = mlp_call(ints, gather_blocks(hm), dys, wg, wu, w_down)
    dh_parts = send_parts(fold_call(ints, dh, shift(dh_its, "core", 1, 2), width), "z")
    g_gu = lax.all_to_all(g_gu, FSDP, 0, 0, tiled=True)
    mid_in, g_gu = lax.optimization_barrier((mid, g_gu))
    d_mid, low, d_o, delta = middle_call(ints, dh_parts, dy, mid_in, gain_m, out_w, o)

    def by_core(partial):
        view = partial.reshape(4, 2, own, -1)
        return lax.dynamic_index_in_dim(view, core, 1, keepdims=False), lax.dynamic_index_in_dim(view, 1 - core, 1, keepdims=False)

    o_mine, o_its = by_core(left_dot(o, low).astype(bf16))
    d_o, o_its = lax.optimization_barrier((d_o, o_its))
    o_recv = shift(o_its, "core", 1, 2)
    out_recv = shift(after(out_its, d_o), "core", 1, 2)
    g_gu, g_down = lax.psum((g_gu, g_down), "x")

    dq, dkv = back_call(ints, q, kv, d_o, lse, delta, own_pos, start, cos, sin)
    owners = lax.all_to_all(dkv.reshape(pairs, rows, 2 * KD), CTX, 0, 0, tiled=True)
    ha_own = lax.dynamic_slice_in_dim(ha_all, me * rows, rows, 0)
    g_kvq = jnp.concatenate([left_dot(ha_all, dkv), left_dot(ha_own, dq[:, :QD])], axis=1).astype(bf16)
    mine, its = by_core(g_kvq)
    g_gu, g_down = lax.psum((after(g_gu, its), after(g_down, its)), "y")
    z_parts = send_parts(turn_call(ints, mine, shift(its, "core", 1, 2), o_mine, after(o_recv, dq)), "z")
    cut = columns_call(ints, z_parts)
    input_grad = last_call(ints, dq, after(owners, cut[0]), w_kvq, x_rows, gain_a, d_mid)
    x_parts = send_parts(cut, "x")
    low_sum = add_parts([after(x_parts[0], input_grad)] + x_parts[1:]).astype(bf16)
    low_sum = add_parts([low_sum] + [shift(low_sum, "y", k) for k in (1, 2, 3)]).astype(bf16)
    out_parts = fold_call(ints, out, after(out_recv, cut[0]), width)
    result = (mid + add_parts(send_parts(out_parts, "z"))).astype(bf16)
    g_key, g_value, g_query, g_out, g_gain_a = finish_call(
        ints, [low_sum] + [shift(low_sum, "x", k) for k in (1, 2, 3)], w_key, w_value, w_query, attn_gain[:, None]
    )
    g_gate, g_up, g_down, g_gain_m = spread_call(ints, after(g_gu, input_grad, result), g_down, w_gate, w_up, mlp_gain[:, None])

    return (
        result.reshape(1, 1, rows, width),
        input_grad.reshape(1, 1, rows, width),
        g_gain_a.reshape(own),
        g_query,
        g_key.T,
        g_value.T,
        g_out,
        g_gain_m.reshape(own),
        g_gate,
        g_up,
        g_down,
    )


def solution(mesh):
    grid = jax.sharding.Mesh(mesh.devices.reshape(4, 4, 4, 2), ("x", "y", "z", "core"))
    tokens = P(CTX, FSDP, None, None)
    vector, matrix = P(FSDP), P(FSDP, None)
    return jax.shard_map(
        per_device,
        mesh=grid,
        in_specs=(tokens, tokens, P(), P(None, FSDP, None), vector, matrix, matrix, matrix, matrix, vector, matrix, matrix, matrix),
        out_specs=(tokens, tokens, vector, matrix, matrix, matrix, matrix, vector, matrix, matrix, matrix),
        check_vma=False,
    )
```

```python
import functools

import jax
import jax.numpy as jnp
import numpy as np
from jax import lax
from jax.experimental import pallas as pl
from jax.experimental.pallas import tpu as pltpu
from jax.sharding import PartitionSpec as P

QUERY_HEADS = 15
KEY_VALUE_HEADS = 5
HEAD_SIZE = 64
GROUP = QUERY_HEADS // KEY_VALUE_HEADS

EPSILON = 1e-05
NEGATIVE = -1e30
ROPE_BASE = 10000.0

CTX = ("x", "y")
FSDP = ("z", "core")
KD = KEY_VALUE_HEADS * HEAD_SIZE
QD = QUERY_HEADS * HEAD_SIZE
PADDED = 1664

bf16, f32 = jnp.bfloat16, jnp.float32
UNROLL, OUTER, INNER, CHUNK, TILE = 5, 5, 1, 1024, 512


def seq_positions(pairing, row_count):
    half_rows = row_count // 2
    count_pairs = pairing.shape[0]
    offsets = jnp.arange(row_count, dtype=jnp.int32)
    early_rows = pairing[:, None] * half_rows + offsets[None, :]
    late_rows = (2 * count_pairs - 1 - pairing[:, None]) * half_rows + offsets[None, :] - half_rows
    return jnp.where(offsets[None, :] < half_rows, early_rows, late_rows)


def rope_tables(length):
    exponent = -(np.arange(HEAD_SIZE // 2, dtype=np.float32) * 2.0) / HEAD_SIZE
    frequency = np.power(ROPE_BASE, exponent.astype(np.float64)).astype(np.float32)
    angles = (np.arange(length, dtype=np.float32)[:, None] * frequency[None, :]).astype(np.float64)
    cos, sin = np.cos(angles).astype(np.float32), np.sin(angles).astype(np.float32)
    return jnp.asarray(np.concatenate([cos] * 4, axis=1)), jnp.asarray(np.concatenate([-sin, sin, -sin, sin], axis=1))


def plain_dot(left, right):
    return jnp.dot(left, right, preferred_element_type=f32)


def left_dot(left, right):
    return lax.dot_general(left, right, (((0,), (0,)), ((), ())), preferred_element_type=f32)


def right_dot(left, right):
    return lax.dot_general(left, right, (((1,), (1,)), ((), ())), preferred_element_type=f32)


def shift(block, axis, step, size=4):
    return lax.ppermute(block, axis, [(i, (i - step) % size) for i in range(size)])


def send_parts(parts, axis):
    return [parts[0]] + [shift(parts[k], axis, -k) for k in (1, 2, 3)]


def add_parts(parts):
    total = parts[0].astype(f32)
    for part in parts[1:]:
        total = total + part.astype(f32)
    return total


def gather_blocks(block):
    blocks = [block] + [shift(block, "z", k) for k in (1, 2, 3)]
    return blocks + [shift(b, "core", 1, 2) for b in blocks]


def after(value, *others):
    return lax.optimization_barrier((value,) + others)[0]


def params(*semantics):
    return pltpu.CompilerParams(vmem_limit_bytes=56 * 2**20)


def cost(flops, read):
    return pl.CostEstimate(flops=1000, bytes_accessed=1000, transcendentals=0)


def swap_halves(value):
    lane = lax.broadcasted_iota(jnp.int32, value.shape, 1)
    return jnp.where(lane % HEAD_SIZE < HEAD_SIZE // 2, pltpu.roll(value, 96, 1), pltpu.roll(value, 32, 1))


def rope(value, cos, sin):
    return value * cos + swap_halves(value) * sin


def rope_keys(value, cos, sin):
    chunks = []
    for j in range(5):
        part = value[:, j * 128 : (j + 1) * 128]
        if j < 2:
            part = rope(part, cos, sin)
        elif j == 2:
            lane = lax.broadcasted_iota(jnp.int32, part.shape, 1)
            part = jnp.where(lane < 64, rope(part, cos, sin), part)
        chunks.append(part)
    return chunks


BLK, X, Y, Z, CORE, ME, SCALARS = 0, 32, 33, 34, 35, 36, 40


def in_smem():
    return pl.BlockSpec(memory_space=pltpu.SMEM)


def in_vmem():
    return pl.BlockSpec(memory_space=pltpu.VMEM)


def call(kernel, name, out_shape, operands, flops=1e9, read=4e6, scratch=()):
    return pl.pallas_call(
        kernel,
        in_specs=[in_smem()] + [in_vmem()] * (len(operands) - 1),
        out_shape=out_shape,
        scratch_shapes=list(scratch),
        compiler_params=params(),
        cost_estimate=cost(flops, read),
        name=name,
    )(*operands)


def shape(dims, dtype=bf16):
    return jax.ShapeDtypeStruct(dims, dtype)


def assemble_kernel(ints, *refs):
    blocks, (w_ref, out_ref, gain_ref, hold) = refs[:8], refs[8:]
    own = blocks[0].shape[0]
    for k in range(4):
        pair = lax.rem(ints[Z] + k, 4) * 2
        hold[pair + ints[CORE]] = blocks[k][...]
        hold[pair + 1 - ints[CORE]] = blocks[4 + k][...]
    for f in range(8):
        w_ref[f * own : (f + 1) * own, :] = hold[f, :, :PADDED]
        out_ref[f * own : (f + 1) * own, :] = hold[f, :, PADDED:]
    gain_ref[...] = jnp.transpose(w_ref[:, PADDED - 128 :].astype(f32))[64:72, :]


def assemble_call(ints, blocks):
    own, columns = blocks[0].shape
    outs = [shape((8 * own, PADDED)), shape((8 * own, columns - PADDED)), shape((8, 8 * own), f32)]
    return call(assemble_kernel, "assemble", outs, [ints, *blocks], scratch=[pltpu.VMEM((8, own, columns), bf16)])


def half_block(ref, ints, number):
    return ref[pl.ds(pl.multiple_of(ints[BLK + number] * 64, 64), 64), :]


def table_rows(ref, ints, first, count):
    return jnp.concatenate([half_block(ref, ints, first + i) for i in range(count)], axis=0)


def qkv_kernel(ints, all_ref, cos_ref, sin_ref, own_ref, w_ref, gain_ref, ha_ref, kv_ref, q_ref):
    i = pl.program_id(0)

    def normed(ref):
        rows = ref[...].astype(f32)
        inv = lax.rsqrt(jnp.mean(rows * rows, axis=1, keepdims=True) + EPSILON)
        return (rows * inv * gain_ref[...]).astype(bf16)

    ha = normed(all_ref)
    ha_ref[...] = ha
    kv = plain_dot(ha, w_ref[:, : 2 * KD])
    blocks = TILE // 64
    cos, sin = table_rows(cos_ref, ints, i * blocks, blocks), table_rows(sin_ref, ints, i * blocks, blocks)
    for j, part in enumerate(rope_keys(kv, cos, sin)):
        part = part.astype(bf16)
        for b in range(blocks):
            at = pl.ds(pl.multiple_of(ints[BLK + i * blocks + b] * 64, 64), 64)
            kv_ref[at, j * 128 : (j + 1) * 128] = part[b * 64 : (b + 1) * 64]

    @pl.when(i == 0)
    def _():
        me = ints[ME]
        own_cos, own_sin = table_rows(cos_ref, ints, me * 2, 2), table_rows(sin_ref, ints, me * 2, 2)
        q = plain_dot(normed(own_ref), w_ref[:, 2 * KD :])
        for j in range(8):
            cols = slice(j * 128, (j + 1) * 128)
            part = rope(q[:, cols], own_cos, own_sin)
            q_ref[:, cols] = (part.astype(bf16).astype(f32) * HEAD_SIZE**-0.5).astype(bf16)


def qkv_call(ints, rows_all, cos, sin, own, w, gain):
    length, width = rows_all.shape
    tile = TILE
    whole = lambda a: pl.BlockSpec(a.shape, lambda i: (0, 0))
    tiled = lambda c: pl.BlockSpec((tile, c), lambda i: (i, 0))
    return pl.pallas_call(
        qkv_kernel,
        grid=(length // tile,),
        in_specs=[in_smem(), tiled(width)] + [whole(a) for a in (cos, sin, own, w, gain)],
        out_specs=[tiled(width), pl.BlockSpec((length, 2 * KD), lambda i: (0, 0)), pl.BlockSpec((own.shape[0], 1024), lambda i: (0, 0))],
        out_shape=[shape((length, width)), shape((length, 2 * KD)), shape((own.shape[0], 1024))],
        compiler_params=params(),
        cost_estimate=cost(3e9, 12e6),
        name="qkv",
    )(ints, rows_all, cos, sin, own, w, gain)


def split_rows(scratch, ref, rows):
    half = rows // 2
    for n in range(QUERY_HEADS):
        h, g = n // GROUP, n % GROUP
        for late in range(2):
            to = ((1 - late) * GROUP + g) * half
            scratch[h, to : to + half, :] = ref[late * half : (late + 1) * half, n * 64 : (n + 1) * 64]


def split_keys(ks, vs, kv_ref):
    for n in range(KEY_VALUE_HEADS):
        ks[n] = kv_ref[:, n * 64 : (n + 1) * 64]
        vs[n] = kv_ref[:, KD + n * 64 : KD + (n + 1) * 64]


def attend_kernel(
    ints, q_ref, kv_ref, qpos_ref, qstart_ref, x_ref, w_ref, gain_ref,
    o_ref, lse_ref, mid_ref, hm_ref, qs, ks, vs, os, bias_early, bias_late, lses,
):
    rows = x_ref.shape[0]
    half, part = rows // 2, GROUP * rows // 2
    split_rows(qs, q_ref, rows)
    split_keys(ks, vs, kv_ref)
    for late, bias in enumerate((bias_early, bias_late)):
        at = slice(late * half, (late + 1) * half)
        kpos = lax.broadcasted_iota(jnp.int32, bias.shape, 1)
        ok = (kpos >= qstart_ref[at, :]) & (qpos_ref[at, :] >= kpos)
        bias[...] = jnp.where(ok, 0.0, NEGATIVE)

    def head(h, carry):
        for late, bias in enumerate((bias_early, bias_late)):
            keys, at = bias.shape[1], slice((1 - late) * part, (2 - late) * part)
            b = bias[...]
            s = right_dot(qs[h, at, :], ks[h, :keys, :]) + jnp.concatenate([b] * GROUP, axis=0)
            top = jnp.max(s, axis=1, keepdims=True)
            p = jnp.exp(s - top)
            total = jnp.sum(p, axis=1, keepdims=True)
            os[h, at, :] = (plain_dot(p.astype(bf16), vs[h, :keys, :]) * (1.0 / total)).astype(bf16)
            lses[h, at, :] = top + jnp.log(total)
        return carry

    lax.fori_loop(0, KEY_VALUE_HEADS, head, 0, unroll=UNROLL)
    for h in range(KEY_VALUE_HEADS):
        lse_ref[h : h + 1, :] = jnp.transpose(jnp.broadcast_to(lses[h], (2 * part, 128)))[:1, :]
    for n in range(QUERY_HEADS):
        h, g = n // GROUP, n % GROUP
        for late in range(2):
            at = ((1 - late) * GROUP + g) * half
            o_ref[late * half : (late + 1) * half, n * 64 : (n + 1) * 64] = os[h, at : at + half, :]
    mid = x_ref[...].astype(f32) + plain_dot(o_ref[...], w_ref[...])
    mid_ref[...] = mid
    inv = lax.rsqrt(jnp.mean(mid * mid, axis=1, keepdims=True) + EPSILON)
    hm_ref[...] = (mid * inv * gain_ref[...]).astype(bf16)


def attend_call(ints, q, kv, qpos, qstart, x, w, gain):
    rows, width = x.shape
    length = kv.shape[0]
    both = GROUP * rows
    return call(
        attend_kernel, "attend",
        [shape((rows, width)), shape((8, both), f32), shape((rows, width), f32), shape((rows, width))],
        [ints, q, kv, qpos, qstart, x, w, gain],
        flops=5e9, read=8e6,
        scratch=[
            pltpu.VMEM((KEY_VALUE_HEADS, both, 64), bf16),
            pltpu.VMEM((KEY_VALUE_HEADS, length, 64), bf16),
            pltpu.VMEM((KEY_VALUE_HEADS, length, 64), bf16),
            pltpu.VMEM((KEY_VALUE_HEADS, both, 64), bf16),
            pltpu.VMEM((rows // 2, length // 2), f32),
            pltpu.VMEM((rows // 2, length), f32),
            pltpu.VMEM((KEY_VALUE_HEADS, both, 1), f32),
        ],
    )


def mlp_kernel(ints, *refs):
    hs, dys = refs[:8], refs[8]
    wg_ref, wu_ref, wd_ref, dh_ref, dh2_ref, out_ref, out2_ref, ggu_ref, gd_ref, all_ref, dy_ref, act_ref, dg_ref, du_ref, hold = refs[9:]
    rows, width = hs[0].shape
    tile = 2 * rows
    for t in range(4):
        at = slice(t * tile, (t + 1) * tile)
        for k in (2 * t, 2 * t + 1):
            all_ref[k * rows : (k + 1) * rows, :] = hs[k][...]
            other = k // 4
            device = lax.rem(ints[Z] + k % 4, 4) * 2 + (1 - ints[CORE] if other else ints[CORE])
            dy_ref[k * rows : (k + 1) * rows, :] = dys[pl.ds(pl.multiple_of(device * rows, rows), rows), :]
        h, dy = all_ref[at, :], dy_ref[at, :]
        gate = plain_dot(h, wg_ref[...])
        up = plain_dot(h, wu_ref[...])
        d_act = right_dot(dy, wd_ref[...])
        sig = jax.nn.sigmoid(gate)
        act = (gate * sig * up).astype(bf16)
        dg = (d_act * up * sig * (1.0 + gate * (1.0 - sig))).astype(bf16)
        du = (d_act * gate * sig).astype(bf16)
        act_ref[at, :] = act
        dg_ref[at, :] = dg
        du_ref[at, :] = du
        to = slice((t % 2) * tile, (t % 2 + 1) * tile)
        first, second = (dh_ref, out_ref) if t < 2 else (dh2_ref, out2_ref)
        first[to, :width] = (right_dot(dg, wg_ref[...]) + right_dot(du, wu_ref[...])).astype(bf16)
        second[to, :width] = plain_dot(act, wd_ref[...]).astype(bf16)
    gd_ref[...] = left_dot(act_ref[...], dy_ref[...]).astype(bf16)
    ff = wg_ref.shape[1]
    for i, ref in enumerate((dg_ref, du_ref)):
        hold[...] = left_dot(all_ref[...], ref[...]).astype(bf16)
        for f in range(8):
            ggu_ref[f, :, i * ff : (i + 1) * ff] = hold[f * (width // 8) : (f + 1) * (width // 8), :]


def mlp_call(ints, hs, dys, wg, wu, wd):
    rows, width = hs[0].shape
    ff = wg.shape[1]
    part = shape((4 * rows, 1024))
    wide, slim = pltpu.VMEM((8 * rows, width), bf16), pltpu.VMEM((8 * rows, ff), bf16)
    return call(
        mlp_kernel, "mlp", [part, part, part, part, shape((8, width // 8, 2 * ff)), shape(wd.shape)],
        [ints, *hs, dys, wg, wu, wd], flops=6e9, read=14e6,
        scratch=[wide, wide, slim, slim, slim, pltpu.VMEM((width, ff), bf16)],
    )


def fold_kernel(ints, mine_ref, its_ref, *parts):
    rows, width = parts[0].shape
    for k, part in enumerate(parts):
        at = slice(k * rows, (k + 1) * rows)
        part[...] = (mine_ref[at, :width].astype(f32) + its_ref[at, :width].astype(f32)).astype(bf16)


def fold_call(ints, mine, its, width):
    rows = mine.shape[0]
    return call(fold_kernel, "fold", [shape((rows // 4, width))] * 4, [ints, mine, its])


def turn_kernel(ints, mine_ref, its_ref, mine2_ref, its2_ref, *parts):
    wide = mine_ref.shape[2]
    for k, part in enumerate(parts):
        at = lax.rem(ints[Z] + k, 4)
        part[:, :wide] = (mine_ref[at].astype(f32) + its_ref[at].astype(f32)).astype(bf16)
        part[:, wide:] = (mine2_ref[at].astype(f32) + its2_ref[at].astype(f32)).astype(bf16)


def turn_call(ints, mine, its, mine2, its2):
    out = shape((mine.shape[1], mine.shape[2] + mine2.shape[2]))
    return call(turn_kernel, "turn", [out] * 4, [ints, mine, its, mine2, its2])


def columns_kernel(ints, *refs):
    given, parts, hold = refs[:4], refs[4:8], refs[8]
    hold[...] = add_parts([r[...] for r in given]).astype(bf16)
    step = parts[0].shape[1]
    for k, part in enumerate(parts):
        part[...] = hold[:, pl.ds(pl.multiple_of(lax.rem(ints[X] + k, 4) * step, 128), step)]


def columns_call(ints, given):
    own, total = given[0].shape
    return call(columns_kernel, "columns", [shape((own, total // 4))] * 4, [ints, *given], scratch=[pltpu.VMEM((own, total), bf16)])


def as_row(column):
    return jnp.transpose(jnp.broadcast_to(column, (column.shape[0], 128)))[:1]


def finish_kernel(ints, p0, p1, p2, p3, wk_ref, wv_ref, wq_ref, gain_ref, k_ref, v_ref, q_ref, o_ref, gain_out, hold):
    step = p0.shape[1]
    for k, part in enumerate((p0, p1, p2, p3)):
        hold[:, pl.ds(pl.multiple_of(lax.rem(ints[X] + k, 4) * step, 128), step)] = part[...]
    k, v = hold[:, :KD].astype(f32), hold[:, KD : 2 * KD].astype(f32)
    q = hold[:, 2 * KD : 2 * KD + QD].astype(f32)
    both = jnp.transpose(hold[:, : 2 * KD].astype(f32))
    k_ref[...], v_ref[...], q_ref[...] = both[:KD], both[KD:], q
    o_ref[...] = hold[:, 2 * KD + QD :].astype(f32)
    total = jnp.sum(q * wq_ref[...].astype(f32), axis=1, keepdims=True)
    total += jnp.sum(k * wk_ref[...].astype(f32), axis=1, keepdims=True) + jnp.sum(v * wv_ref[...].astype(f32), axis=1, keepdims=True)
    gain_out[...] = as_row(total / gain_ref[...].astype(f32))


def finish_call(ints, parts, wk, wv, wq, gain):
    own = wk.shape[0]
    return call(
        finish_kernel, "finish",
        [shape((KD, own), f32), shape((KD, own), f32), shape((own, QD), f32), shape((own, QD), f32), shape((1, own), f32)],
        [ints, *parts, wk, wv, wq, gain],
        scratch=[pltpu.VMEM((own, 2 * KD + 2 * QD), bf16)],
    )


def spread_kernel(ints, g_ref, d_ref, wg_ref, wu_ref, gain_ref, gate_ref, up_ref, down_ref, gain_out):
    ff = g_ref.shape[2] // 2
    for f in range(8):
        gate_ref[:, f * ff : (f + 1) * ff] = g_ref[f, :, :ff].astype(f32)
        up_ref[:, f * ff : (f + 1) * ff] = g_ref[f, :, ff:].astype(f32)
    down_ref[...] = d_ref[...].astype(f32)
    total = jnp.sum(gate_ref[...] * wg_ref[...].astype(f32), axis=1, keepdims=True)
    total += jnp.sum(up_ref[...] * wu_ref[...].astype(f32), axis=1, keepdims=True)
    gain_out[...] = as_row(total / gain_ref[...].astype(f32))


def spread_call(ints, g, d, wg, wu, gain):
    wide = shape(wg.shape, f32)
    return call(spread_kernel, "spread", [wide, wide, shape(d.shape, f32), shape((1, wg.shape[0]), f32)], [ints, g, d, wg, wu, gain])


def norm_back(grad_normed, normed, inv_rms, gain):
    scaled = grad_normed * gain
    return inv_rms * (scaled - normed * jnp.mean(scaled * normed, axis=1, keepdims=True))


def middle_kernel(ints, d0, d1, d2, d3, dy_ref, mid_ref, gain_ref, w_ref, o_ref, dmid_ref, low_ref, do_ref, delta_ref):
    rows = mid_ref.shape[0]
    d_hm = add_parts([d0[...], d1[...], d2[...], d3[...]])
    mid = mid_ref[...]
    inv = lax.rsqrt(jnp.mean(mid * mid, axis=1, keepdims=True) + EPSILON)
    d_mid = dy_ref[...].astype(f32) + norm_back(d_hm, mid * inv, inv, gain_ref[...])
    dmid_ref[...] = d_mid
    low = d_mid.astype(bf16)
    low_ref[...] = low
    d_o = right_dot(low, w_ref[...]).astype(bf16)
    do_ref[...] = d_o
    prod = d_o.astype(f32) * o_ref[...].astype(f32)
    half = rows // 2
    for h in range(KEY_VALUE_HEADS):
        ones = [jnp.sum(prod[:, n * 64 : (n + 1) * 64], axis=1, keepdims=True) for n in range(h * GROUP, (h + 1) * GROUP)]
        column = jnp.concatenate([one[half:] for one in ones] + [one[:half] for one in ones], axis=0)
        delta_ref[h : h + 1, :] = jnp.transpose(jnp.broadcast_to(column, (GROUP * rows, 128)))[:1, :]


def middle_call(ints, parts, dy, mid, gain, w, o):
    rows, width = mid.shape
    return call(
        middle_kernel, "middle",
        [shape((rows, width), f32), shape((rows, width)), shape((rows, width)), shape((8, GROUP * rows), f32)],
        [ints, *parts, dy, mid, gain, w, o],
    )


def back_kernel(ints, q_ref, kv_ref, do_ref, lse_ref, delta_ref, qpos_ref, qstart_ref, cos_ref, sin_ref, dq_ref, dkv_ref, qs, ds, ks, vs, dks, dvs, dqs, bias):
    rows, length = do_ref.shape[0], kv_ref.shape[0]
    chunk = CHUNK
    half, part = rows // 2, GROUP * rows // 2
    split_rows(qs, q_ref, rows)
    split_rows(ds, do_ref, rows)
    split_keys(ks, vs, kv_ref)
    kpos = lax.broadcasted_iota(jnp.int32, (length, rows), 0)
    ok = (kpos >= qstart_ref[...]) & (qpos_ref[...] >= kpos)
    allowed = jnp.where(ok, 0.0, NEGATIVE)
    bias[...] = jnp.concatenate([allowed[:, half:]] * GROUP + [allowed[:, :half]] * GROUP, axis=1)

    def head(h, carry):
        lse, delta = lse_ref[pl.ds(h, 1), :], delta_ref[pl.ds(h, 1), :]

        def step(c, dq, columns):
            at = pl.ds(pl.multiple_of(c * chunk, chunk), chunk)
            q, d = qs[h, :columns, :], ds[h, :columns, :]
            k, v = ks[h, at, :], vs[h, at, :]
            p = jnp.exp(right_dot(k, q) + bias[at, :columns] - lse[:, :columns])
            dp = right_dot(v, d)
            low = p.astype(bf16)
            dscore = (p * (dp - delta[:, :columns])).astype(bf16)
            dvs[h, at, :] = plain_dot(low, d)
            dks[h, at, :] = plain_dot(dscore, q)
            return dq + left_dot(k, dscore)

        n = length // chunk
        both = GROUP * rows
        dqs[h] = lax.fori_loop(0, n // 2, functools.partial(step, columns=both), jnp.zeros((64, both), f32), unroll=INNER)
        late = lax.fori_loop(n // 2, n, functools.partial(step, columns=part), jnp.zeros((64, part), f32), unroll=INNER)
        dqs[h, :, :part] = dqs[h, :, :part] + late
        return carry

    lax.fori_loop(0, KEY_VALUE_HEADS, head, 0, unroll=OUTER)
    me = ints[ME]
    own_cos, own_sin = table_rows(cos_ref, ints, me * 2, 2), -table_rows(sin_ref, ints, me * 2, 2)
    scale = HEAD_SIZE**-0.5
    for j in range(8):
        pieces = []
        for n in (2 * j, 2 * j + 1):
            n = min(n, QUERY_HEADS - 1)
            h, g = n // GROUP, n % GROUP
            pieces.append(jnp.concatenate([dqs[h, :, ((1 - late) * GROUP + g) * half : ((1 - late) * GROUP + g + 1) * half] for late in range(2)], axis=1))
        part = jnp.transpose(jnp.concatenate(pieces, axis=0)) * scale
        dq_ref[:, j * 128 : (j + 1) * 128] = rope(part, own_cos, own_sin).astype(bf16)

    def finish(t, carry):
        at = pl.ds(pl.multiple_of(t * 256, 256), 256)
        rows_of = lambda ref, n: jnp.concatenate([half_block(ref.at[n], ints, t * 4 + i) for i in range(4)], axis=0)
        both = [rows_of(dks, n) for n in range(KEY_VALUE_HEADS)] + [rows_of(dvs, n) for n in range(KEY_VALUE_HEADS)]
        both = jnp.concatenate(both, axis=1)
        cos, sin = table_rows(cos_ref, ints, t * 4, 4), -table_rows(sin_ref, ints, t * 4, 4)
        for j, part in enumerate(rope_keys(both, cos, sin)):
            dkv_ref[at, j * 128 : (j + 1) * 128] = part.astype(bf16)
        return carry

    lax.fori_loop(0, length // 256, finish, 0)


def back_call(ints, q, kv, d_o, lse, delta, qpos, qstart, cos, sin):
    rows, length = d_o.shape[0], kv.shape[0]
    both = GROUP * rows
    heads = KEY_VALUE_HEADS
    return call(
        back_kernel, "back",
        [shape((rows, 1024)), shape((length, 2 * KD))],
        [ints, q, kv, d_o, lse, delta, qpos, qstart, cos, sin],
        flops=20e9, read=8e6,
        scratch=[
            pltpu.VMEM((heads, both, 64), bf16),
            pltpu.VMEM((heads, both, 64), bf16),
            pltpu.VMEM((heads, length, 64), bf16),
            pltpu.VMEM((heads, length, 64), bf16),
            pltpu.VMEM((heads, length, 64), f32),
            pltpu.VMEM((heads, length, 64), f32),
            pltpu.VMEM((heads, 64, both), f32),
            pltpu.VMEM((length, both), f32),
        ],
    )


def last_kernel(ints, dq_ref, parts_ref, w_ref, x_ref, gain_ref, dmid_ref, out_ref):
    dkv = add_parts([parts_ref[c] for c in range(parts_ref.shape[0])]).astype(bf16)
    d_ha = right_dot(dkv, w_ref[:, : 2 * KD]) + right_dot(dq_ref[:, :QD], w_ref[:, 2 * KD : 2 * KD + QD])
    x = x_ref[...].astype(f32)
    inv = lax.rsqrt(jnp.mean(x * x, axis=1, keepdims=True) + EPSILON)
    out_ref[...] = (dmid_ref[...] + norm_back(d_ha, x * inv, inv, gain_ref[...])).astype(bf16)


def last_call(ints, dq, parts, w, x, gain, d_mid):
    return call(last_kernel, "last", shape(x.shape), [ints, dq, parts, w, x, gain, d_mid])


def per_device(
    hidden,
    cotangent,
    pairing,
    documents,
    attn_gain,
    w_query,
    w_key,
    w_value,
    w_out,
    mlp_gain,
    w_gate,
    w_up,
    w_down,
):
    rows, width = hidden.shape[2:]
    own = width // 8
    ff = w_gate.shape[1] // 8
    x, y, z, core = (lax.axis_index(name) for name in ("x", "y", "z", "core"))
    me = x * 4 + y
    pairs = pairing.shape[0]
    x_rows = hidden.reshape(rows, width)
    dy = cotangent.reshape(rows, width)

    rows_all = lax.all_gather(x_rows, CTX, axis=0, tiled=True)
    blocks = jnp.stack([pairing, 2 * pairs - 1 - pairing], axis=1).reshape(-1)
    ints = jnp.concatenate([blocks, jnp.stack([x, y, z, core, me, me, me, me]).astype(jnp.int32)])
    shard = jnp.concatenate(
        [w_key, w_value, w_query, attn_gain[:, None], mlp_gain[:, None], jnp.zeros((own, PADDED - 2 * KD - QD - 2), bf16), w_out], axis=1
    )
    w_kvq, out_w, gains = assemble_call(ints, gather_blocks(shard))
    dys = lax.all_gather(after(dy, w_kvq), FSDP, axis=0, tiled=True)
    gain_a, gain_m = gains[:1], gains[1:2]
    positions = seq_positions(pairing, rows)
    docs = documents[:, 0, :]
    own_pos = lax.dynamic_index_in_dim(positions, me, 0)
    own_doc = lax.dynamic_index_in_dim(docs, me, 0)
    start = jnp.sum((docs.reshape(-1, 1) < own_doc).astype(jnp.int32), axis=0, keepdims=True)
    cos, sin = rope_tables(2 * pairs * 64)
    gate_up = jnp.concatenate([w_gate.reshape(own, 8, ff), w_up.reshape(own, 8, ff)], axis=2).transpose(1, 0, 2)
    gate_up = lax.all_to_all(gate_up, FSDP, 0, 0, tiled=True).reshape(width, 2 * ff)
    wg, wu = gate_up[:, :ff], gate_up[:, ff:]
    rows_all, w_kvq, start, out_w = lax.optimization_barrier((rows_all, w_kvq, start, out_w))

    ha_all, kv, q = qkv_call(ints, rows_all, cos, sin, x_rows, w_kvq, gain_a)
    o, lse, mid, hm = attend_call(
        ints, q, kv, own_pos.reshape(-1, 1), start.reshape(-1, 1), x_rows, out_w, gain_m
    )

    dh, dh_its, out, out_its, g_gu, g_down = mlp_call(ints, gather_blocks(hm), dys, wg, wu, w_down)
    dh_parts = send_parts(fold_call(ints, dh, shift(dh_its, "core", 1, 2), width), "z")
    g_gu = lax.all_to_all(g_gu, FSDP, 0, 0, tiled=True)
    mid_in, g_gu = lax.optimization_barrier((mid, g_gu))
    d_mid, low, d_o, delta = middle_call(ints, dh_parts, dy, mid_in, gain_m, out_w, o)

    def by_core(partial):
        view = partial.reshape(4, 2, own, -1)
        return lax.dynamic_index_in_dim(view, core, 1, keepdims=False), lax.dynamic_index_in_dim(view, 1 - core, 1, keepdims=False)

    o_mine, o_its = by_core(left_dot(o, low).astype(bf16))
    d_o, o_its = lax.optimization_barrier((d_o, o_its))
    o_recv = shift(o_its, "core", 1, 2)
    out_recv = shift(after(out_its, d_o), "core", 1, 2)
    g_gu, g_down = lax.psum((g_gu, g_down), "x")

    dq, dkv = back_call(ints, q, kv, d_o, lse, delta, own_pos, start, cos, sin)
    ha_own = lax.dynamic_slice_in_dim(ha_all, me * rows, rows, 0)
    g_kvq = jnp.concatenate([left_dot(ha_all, dkv), left_dot(ha_own, dq[:, :QD])], axis=1).astype(bf16)
    mine, its = by_core(g_kvq)
    turned = turn_call(ints, mine, shift(its, "core", 1, 2), o_mine, after(o_recv, dq))
    g_gu, g_down = after(g_gu, turned[0]), after(g_down, turned[0])
    owners = lax.all_to_all(after(dkv, g_gu).reshape(pairs, rows, 2 * KD), CTX, 0, 0, tiled=True)
    g_gu, g_down = lax.psum((g_gu, g_down), "y")
    z_parts = send_parts(turned, "z")
    cut = columns_call(ints, z_parts)
    input_grad = last_call(ints, dq, after(owners, cut[0]), w_kvq, x_rows, gain_a, d_mid)
    x_parts = send_parts(cut, "x")
    low_sum = add_parts([after(x_parts[0], input_grad)] + x_parts[1:]).astype(bf16)
    low_sum = add_parts([low_sum] + [shift(low_sum, "y", k) for k in (1, 2, 3)]).astype(bf16)
    out_parts = fold_call(ints, out, after(out_recv, cut[0]), width)
    result = (mid + add_parts(send_parts(out_parts, "z"))).astype(bf16)
    g_key, g_value, g_query, g_out, g_gain_a = finish_call(
        ints, [low_sum] + [shift(low_sum, "x", k) for k in (1, 2, 3)], w_key, w_value, w_query, attn_gain[:, None]
    )
    g_gate, g_up, g_down, g_gain_m = spread_call(ints, after(g_gu, low_sum), g_down, w_gate, w_up, mlp_gain[:, None])

    return (
        result.reshape(1, 1, rows, width),
        input_grad.reshape(1, 1, rows, width),
        g_gain_a.reshape(own),
        g_query,
        g_key.T,
        g_value.T,
        g_out,
        g_gain_m.reshape(own),
        g_gate,
        g_up,
        g_down,
    )


def solution(mesh):
    grid = jax.sharding.Mesh(mesh.devices.reshape(4, 4, 4, 2), ("x", "y", "z", "core"))
    tokens = P(CTX, FSDP, None, None)
    vector, matrix = P(FSDP), P(FSDP, None)
    return jax.shard_map(
        per_device,
        mesh=grid,
        in_specs=(tokens, tokens, P(), P(None, FSDP, None), vector, matrix, matrix, matrix, matrix, vector, matrix, matrix, matrix),
        out_specs=(tokens, tokens, vector, matrix, matrix, matrix, matrix, vector, matrix, matrix, matrix),
        check_vma=False,
    )
```

```python
import functools

import jax
import jax.numpy as jnp
import numpy as np
from jax import lax
from jax.experimental import pallas as pl
from jax.experimental.pallas import tpu as pltpu
from jax.sharding import PartitionSpec as P

QUERY_HEADS = 15
KEY_VALUE_HEADS = 5
HEAD_SIZE = 64
GROUP = QUERY_HEADS // KEY_VALUE_HEADS

EPSILON = 1e-05
NEGATIVE = -1e30
ROPE_BASE = 10000.0

CTX = ("x", "y")
FSDP = ("z", "core")
KD = KEY_VALUE_HEADS * HEAD_SIZE
QD = QUERY_HEADS * HEAD_SIZE
PADDED = 1664

bf16, f32 = jnp.bfloat16, jnp.float32
UNROLL, OUTER, INNER, CHUNK, TILE = 5, 5, 1, 1024, 512


def seq_positions(pairing, row_count):
    half_rows = row_count // 2
    count_pairs = pairing.shape[0]
    offsets = jnp.arange(row_count, dtype=jnp.int32)
    early_rows = pairing[:, None] * half_rows + offsets[None, :]
    late_rows = (2 * count_pairs - 1 - pairing[:, None]) * half_rows + offsets[None, :] - half_rows
    return jnp.where(offsets[None, :] < half_rows, early_rows, late_rows)


def rope_tables(length):
    exponent = -(np.arange(HEAD_SIZE // 2, dtype=np.float32) * 2.0) / HEAD_SIZE
    frequency = np.power(ROPE_BASE, exponent.astype(np.float64)).astype(np.float32)
    angles = (np.arange(length, dtype=np.float32)[:, None] * frequency[None, :]).astype(np.float64)
    cos, sin = np.cos(angles).astype(np.float32), np.sin(angles).astype(np.float32)
    return jnp.asarray(np.concatenate([cos] * 4, axis=1)), jnp.asarray(np.concatenate([-sin, sin, -sin, sin], axis=1))


def plain_dot(left, right):
    return jnp.dot(left, right, preferred_element_type=f32)


def left_dot(left, right):
    return lax.dot_general(left, right, (((0,), (0,)), ((), ())), preferred_element_type=f32)


def right_dot(left, right):
    return lax.dot_general(left, right, (((1,), (1,)), ((), ())), preferred_element_type=f32)


def shift(block, axis, step, size=4):
    return lax.ppermute(block, axis, [(i, (i - step) % size) for i in range(size)])


def send_parts(parts, axis):
    return [parts[0]] + [shift(parts[k], axis, -k) for k in (1, 2, 3)]


def add_parts(parts):
    total = parts[0].astype(f32)
    for part in parts[1:]:
        total = total + part.astype(f32)
    return total


def gather_blocks(block):
    blocks = [block] + [shift(block, "z", k) for k in (1, 2, 3)]
    return blocks + [shift(b, "core", 1, 2) for b in blocks]


def after(value, *others):
    return lax.optimization_barrier((value,) + others)[0]


def params(*semantics):
    return pltpu.CompilerParams(vmem_limit_bytes=56 * 2**20)


def cost(flops, read):
    return pl.CostEstimate(flops=1000, bytes_accessed=1000, transcendentals=0)


def swap_halves(value):
    lane = lax.broadcasted_iota(jnp.int32, value.shape, 1)
    return jnp.where(lane % HEAD_SIZE < HEAD_SIZE // 2, pltpu.roll(value, 96, 1), pltpu.roll(value, 32, 1))


def rope(value, cos, sin):
    return value * cos + swap_halves(value) * sin


def rope_keys(value, cos, sin):
    chunks = []
    for j in range(5):
        part = value[:, j * 128 : (j + 1) * 128]
        if j < 2:
            part = rope(part, cos, sin)
        elif j == 2:
            lane = lax.broadcasted_iota(jnp.int32, part.shape, 1)
            part = jnp.where(lane < 64, rope(part, cos, sin), part)
        chunks.append(part)
    return chunks


BLK, X, Y, Z, CORE, ME, SCALARS = 0, 32, 33, 34, 35, 36, 40


def in_smem():
    return pl.BlockSpec(memory_space=pltpu.SMEM)


def in_vmem():
    return pl.BlockSpec(memory_space=pltpu.VMEM)


def call(kernel, name, out_shape, operands, flops=1e9, read=4e6, scratch=()):
    return pl.pallas_call(
        kernel,
        in_specs=[in_smem()] + [in_vmem()] * (len(operands) - 1),
        out_shape=out_shape,
        scratch_shapes=list(scratch),
        compiler_params=params(),
        cost_estimate=cost(flops, read),
        name=name,
    )(*operands)


def shape(dims, dtype=bf16):
    return jax.ShapeDtypeStruct(dims, dtype)


def assemble_kernel(ints, *refs):
    blocks, (w_ref, out_ref, gain_ref, hold) = refs[:8], refs[8:]
    own = blocks[0].shape[0]
    for k in range(4):
        pair = lax.rem(ints[Z] + k, 4) * 2
        hold[pair + ints[CORE]] = blocks[k][...]
        hold[pair + 1 - ints[CORE]] = blocks[4 + k][...]
    for f in range(8):
        w_ref[f * own : (f + 1) * own, :] = hold[f, :, :PADDED]
        out_ref[f * own : (f + 1) * own, :] = hold[f, :, PADDED:]
    gain_ref[...] = jnp.transpose(w_ref[:, PADDED - 128 :].astype(f32))[64:72, :]


def assemble_call(ints, blocks):
    own, columns = blocks[0].shape
    outs = [shape((8 * own, PADDED)), shape((8 * own, columns - PADDED)), shape((8, 8 * own), f32)]
    return call(assemble_kernel, "assemble", outs, [ints, *blocks], scratch=[pltpu.VMEM((8, own, columns), bf16)])


def half_block(ref, ints, number):
    return ref[pl.ds(pl.multiple_of(ints[BLK + number] * 64, 64), 64), :]


def table_rows(ref, ints, first, count):
    return jnp.concatenate([half_block(ref, ints, first + i) for i in range(count)], axis=0)


def qkv_kernel(ints, all_ref, cos_ref, sin_ref, own_ref, w_ref, gain_ref, ha_ref, kv_ref, q_ref):
    i = pl.program_id(0)

    def normed(ref):
        rows = ref[...].astype(f32)
        inv = lax.rsqrt(jnp.mean(rows * rows, axis=1, keepdims=True) + EPSILON)
        return (rows * inv * gain_ref[...]).astype(bf16)

    ha = normed(all_ref)
    ha_ref[...] = ha
    kv = plain_dot(ha, w_ref[:, : 2 * KD])
    blocks = TILE // 64
    cos, sin = table_rows(cos_ref, ints, i * blocks, blocks), table_rows(sin_ref, ints, i * blocks, blocks)
    for j, part in enumerate(rope_keys(kv, cos, sin)):
        part = part.astype(bf16)
        for b in range(blocks):
            at = pl.ds(pl.multiple_of(ints[BLK + i * blocks + b] * 64, 64), 64)
            kv_ref[at, j * 128 : (j + 1) * 128] = part[b * 64 : (b + 1) * 64]

    @pl.when(i == 0)
    def _():
        me = ints[ME]
        own_cos, own_sin = table_rows(cos_ref, ints, me * 2, 2), table_rows(sin_ref, ints, me * 2, 2)
        q = plain_dot(normed(own_ref), w_ref[:, 2 * KD :])
        for j in range(8):
            cols = slice(j * 128, (j + 1) * 128)
            part = rope(q[:, cols], own_cos, own_sin)
            q_ref[:, cols] = (part.astype(bf16).astype(f32) * HEAD_SIZE**-0.5).astype(bf16)


def qkv_call(ints, rows_all, cos, sin, own, w, gain):
    length, width = rows_all.shape
    tile = TILE
    whole = lambda a: pl.BlockSpec(a.shape, lambda i: (0, 0))
    tiled = lambda c: pl.BlockSpec((tile, c), lambda i: (i, 0))
    return pl.pallas_call(
        qkv_kernel,
        grid=(length // tile,),
        in_specs=[in_smem(), tiled(width)] + [whole(a) for a in (cos, sin, own, w, gain)],
        out_specs=[tiled(width), pl.BlockSpec((length, 2 * KD), lambda i: (0, 0)), pl.BlockSpec((own.shape[0], 1024), lambda i: (0, 0))],
        out_shape=[shape((length, width)), shape((length, 2 * KD)), shape((own.shape[0], 1024))],
        compiler_params=params(),
        cost_estimate=cost(3e9, 12e6),
        name="qkv",
    )(ints, rows_all, cos, sin, own, w, gain)


def split_rows(scratch, ref, rows):
    half = rows // 2
    for n in range(QUERY_HEADS):
        h, g = n // GROUP, n % GROUP
        for late in range(2):
            to = ((1 - late) * GROUP + g) * half
            scratch[h, to : to + half, :] = ref[late * half : (late + 1) * half, n * 64 : (n + 1) * 64]


def split_keys(ks, vs, kv_ref):
    for n in range(KEY_VALUE_HEADS):
        ks[n] = kv_ref[:, n * 64 : (n + 1) * 64]
        vs[n] = kv_ref[:, KD + n * 64 : KD + (n + 1) * 64]


def attend_kernel(
    ints, q_ref, kv_ref, qpos_ref, qstart_ref, x_ref, w_ref, gain_ref,
    o_ref, lse_ref, mid_ref, hm_ref, qs, ks, vs, os, bias_early, bias_late, lses,
):
    rows = x_ref.shape[0]
    half, part = rows // 2, GROUP * rows // 2
    split_rows(qs, q_ref, rows)
    split_keys(ks, vs, kv_ref)
    for late, bias in enumerate((bias_early, bias_late)):
        at = slice(late * half, (late + 1) * half)
        kpos = lax.broadcasted_iota(jnp.int32, bias.shape, 1)
        ok = (kpos >= qstart_ref[at, :]) & (qpos_ref[at, :] >= kpos)
        bias[...] = jnp.where(ok, 0.0, NEGATIVE)

    def head(h, carry):
        for late, bias in enumerate((bias_early, bias_late)):
            keys, at = bias.shape[1], slice((1 - late) * part, (2 - late) * part)
            b = bias[...]
            s = right_dot(qs[h, at, :], ks[h, :keys, :]) + jnp.concatenate([b] * GROUP, axis=0)
            top = jnp.max(s, axis=1, keepdims=True)
            p = jnp.exp(s - top)
            total = jnp.sum(p, axis=1, keepdims=True)
            os[h, at, :] = (plain_dot(p.astype(bf16), vs[h, :keys, :]) * (1.0 / total)).astype(bf16)
            lses[h, at, :] = top + jnp.log(total)
        return carry

    lax.fori_loop(0, KEY_VALUE_HEADS, head, 0, unroll=UNROLL)
    for h in range(KEY_VALUE_HEADS):
        lse_ref[h : h + 1, :] = jnp.transpose(jnp.broadcast_to(lses[h], (2 * part, 128)))[:1, :]
    for n in range(QUERY_HEADS):
        h, g = n // GROUP, n % GROUP
        for late in range(2):
            at = ((1 - late) * GROUP + g) * half
            o_ref[late * half : (late + 1) * half, n * 64 : (n + 1) * 64] = os[h, at : at + half, :]
    mid = x_ref[...].astype(f32) + plain_dot(o_ref[...], w_ref[...])
    mid_ref[...] = mid
    inv = lax.rsqrt(jnp.mean(mid * mid, axis=1, keepdims=True) + EPSILON)
    hm_ref[...] = (mid * inv * gain_ref[...]).astype(bf16)


def attend_call(ints, q, kv, qpos, qstart, x, w, gain):
    rows, width = x.shape
    length = kv.shape[0]
    both = GROUP * rows
    return call(
        attend_kernel, "attend",
        [shape((rows, width)), shape((8, both), f32), shape((rows, width), f32), shape((rows, width))],
        [ints, q, kv, qpos, qstart, x, w, gain],
        flops=5e9, read=8e6,
        scratch=[
            pltpu.VMEM((KEY_VALUE_HEADS, both, 64), bf16),
            pltpu.VMEM((KEY_VALUE_HEADS, length, 64), bf16),
            pltpu.VMEM((KEY_VALUE_HEADS, length, 64), bf16),
            pltpu.VMEM((KEY_VALUE_HEADS, both, 64), bf16),
            pltpu.VMEM((rows // 2, length // 2), f32),
            pltpu.VMEM((rows // 2, length), f32),
            pltpu.VMEM((KEY_VALUE_HEADS, both, 1), f32),
        ],
    )


def mlp_kernel(ints, *refs):
    hs, dys = refs[:8], refs[8]
    wg_ref, wu_ref, wd_ref, dh_ref, dh2_ref, out_ref, out2_ref, ggu_ref, gd_ref, all_ref, dy_ref, act_ref, dg_ref, du_ref, hold = refs[9:]
    rows, width = hs[0].shape
    tile = 2 * rows
    for t in range(4):
        at = slice(t * tile, (t + 1) * tile)
        for k in (2 * t, 2 * t + 1):
            all_ref[k * rows : (k + 1) * rows, :] = hs[k][...]
            other = k // 4
            device = lax.rem(ints[Z] + k % 4, 4) * 2 + (1 - ints[CORE] if other else ints[CORE])
            dy_ref[k * rows : (k + 1) * rows, :] = dys[pl.ds(pl.multiple_of(device * rows, rows), rows), :]
        h, dy = all_ref[at, :], dy_ref[at, :]
        gate = plain_dot(h, wg_ref[...])
        up = plain_dot(h, wu_ref[...])
        d_act = right_dot(dy, wd_ref[...])
        sig = jax.nn.sigmoid(gate)
        act = (gate * sig * up).astype(bf16)
        dg = (d_act * up * sig * (1.0 + gate * (1.0 - sig))).astype(bf16)
        du = (d_act * gate * sig).astype(bf16)
        act_ref[at, :] = act
        dg_ref[at, :] = dg
        du_ref[at, :] = du
        to = slice((t % 2) * tile, (t % 2 + 1) * tile)
        first, second = (dh_ref, out_ref) if t < 2 else (dh2_ref, out2_ref)
        first[to, :width] = (right_dot(dg, wg_ref[...]) + right_dot(du, wu_ref[...])).astype(bf16)
        second[to, :width] = plain_dot(act, wd_ref[...]).astype(bf16)
    gd_ref[...] = left_dot(act_ref[...], dy_ref[...]).astype(bf16)
    ff = wg_ref.shape[1]
    for i, ref in enumerate((dg_ref, du_ref)):
        hold[...] = left_dot(all_ref[...], ref[...]).astype(bf16)
        for f in range(8):
            ggu_ref[f, :, i * ff : (i + 1) * ff] = hold[f * (width // 8) : (f + 1) * (width // 8), :]


def mlp_call(ints, hs, dys, wg, wu, wd):
    rows, width = hs[0].shape
    ff = wg.shape[1]
    part = shape((4 * rows, 1024))
    wide, slim = pltpu.VMEM((8 * rows, width), bf16), pltpu.VMEM((8 * rows, ff), bf16)
    return call(
        mlp_kernel, "mlp", [part, part, part, part, shape((8, width // 8, 2 * ff)), shape(wd.shape)],
        [ints, *hs, dys, wg, wu, wd], flops=6e9, read=14e6,
        scratch=[wide, wide, slim, slim, slim, pltpu.VMEM((width, ff), bf16)],
    )


def fold_kernel(ints, mine_ref, its_ref, *parts):
    rows, width = parts[0].shape
    for k, part in enumerate(parts):
        at = slice(k * rows, (k + 1) * rows)
        part[...] = (mine_ref[at, :width].astype(f32) + its_ref[at, :width].astype(f32)).astype(bf16)


def fold_call(ints, mine, its, width):
    rows = mine.shape[0]
    return call(fold_kernel, "fold", [shape((rows // 4, width))] * 4, [ints, mine, its])


def turn_kernel(ints, mine_ref, its_ref, mine2_ref, its2_ref, *parts):
    wide = mine_ref.shape[2]
    for k, part in enumerate(parts):
        at = lax.rem(ints[Z] + k, 4)
        part[:, :wide] = (mine_ref[at].astype(f32) + its_ref[at].astype(f32)).astype(bf16)
        part[:, wide:] = (mine2_ref[at].astype(f32) + its2_ref[at].astype(f32)).astype(bf16)


def turn_call(ints, mine, its, mine2, its2):
    out = shape((mine.shape[1], mine.shape[2] + mine2.shape[2]))
    return call(turn_kernel, "turn", [out] * 4, [ints, mine, its, mine2, its2])


def columns_kernel(ints, *refs):
    given, parts, hold = refs[:4], refs[4:8], refs[8]
    hold[...] = add_parts([r[...] for r in given]).astype(bf16)
    step = parts[0].shape[1]
    for k, part in enumerate(parts):
        part[...] = hold[:, pl.ds(pl.multiple_of(lax.rem(ints[X] + k, 4) * step, 128), step)]


def columns_call(ints, given):
    own, total = given[0].shape
    return call(columns_kernel, "columns", [shape((own, total // 4))] * 4, [ints, *given], scratch=[pltpu.VMEM((own, total), bf16)])


def as_row(column):
    return jnp.transpose(jnp.broadcast_to(column, (column.shape[0], 128)))[:1]


def finish_kernel(ints, p0, p1, p2, p3, wk_ref, wv_ref, wq_ref, gain_ref, k_ref, v_ref, q_ref, o_ref, gain_out, hold):
    step = p0.shape[1]
    for k, part in enumerate((p0, p1, p2, p3)):
        hold[:, pl.ds(pl.multiple_of(lax.rem(ints[X] + k, 4) * step, 128), step)] = part[...]
    k, v = hold[:, :KD].astype(f32), hold[:, KD : 2 * KD].astype(f32)
    q = hold[:, 2 * KD : 2 * KD + QD].astype(f32)
    both = jnp.transpose(hold[:, : 2 * KD].astype(f32))
    k_ref[...], v_ref[...], q_ref[...] = both[:KD], both[KD:], q
    o_ref[...] = hold[:, 2 * KD + QD :].astype(f32)
    total = jnp.sum(q * wq_ref[...].astype(f32), axis=1, keepdims=True)
    total += jnp.sum(k * wk_ref[...].astype(f32), axis=1, keepdims=True) + jnp.sum(v * wv_ref[...].astype(f32), axis=1, keepdims=True)
    gain_out[...] = as_row(total / gain_ref[...].astype(f32))


def finish_call(ints, parts, wk, wv, wq, gain):
    own = wk.shape[0]
    return call(
        finish_kernel, "finish",
        [shape((KD, own), f32), shape((KD, own), f32), shape((own, QD), f32), shape((own, QD), f32), shape((1, own), f32)],
        [ints, *parts, wk, wv, wq, gain],
        scratch=[pltpu.VMEM((own, 2 * KD + 2 * QD), bf16)],
    )


def spread_kernel(ints, g_ref, d_ref, wg_ref, wu_ref, gain_ref, gate_ref, up_ref, down_ref, gain_out):
    ff = g_ref.shape[2] // 2
    for f in range(8):
        gate_ref[:, f * ff : (f + 1) * ff] = g_ref[f, :, :ff].astype(f32)
        up_ref[:, f * ff : (f + 1) * ff] = g_ref[f, :, ff:].astype(f32)
    down_ref[...] = d_ref[...].astype(f32)
    total = jnp.sum(gate_ref[...] * wg_ref[...].astype(f32), axis=1, keepdims=True)
    total += jnp.sum(up_ref[...] * wu_ref[...].astype(f32), axis=1, keepdims=True)
    gain_out[...] = as_row(total / gain_ref[...].astype(f32))


def spread_call(ints, g, d, wg, wu, gain):
    wide = shape(wg.shape, f32)
    return call(spread_kernel, "spread", [wide, wide, shape(d.shape, f32), shape((1, wg.shape[0]), f32)], [ints, g, d, wg, wu, gain])


def norm_back(grad_normed, normed, inv_rms, gain):
    scaled = grad_normed * gain
    return inv_rms * (scaled - normed * jnp.mean(scaled * normed, axis=1, keepdims=True))


def middle_kernel(ints, d0, d1, d2, d3, dy_ref, mid_ref, gain_ref, w_ref, o_ref, dmid_ref, low_ref, do_ref, delta_ref):
    rows = mid_ref.shape[0]
    d_hm = add_parts([d0[...], d1[...], d2[...], d3[...]])
    mid = mid_ref[...]
    inv = lax.rsqrt(jnp.mean(mid * mid, axis=1, keepdims=True) + EPSILON)
    d_mid = dy_ref[...].astype(f32) + norm_back(d_hm, mid * inv, inv, gain_ref[...])
    dmid_ref[...] = d_mid
    low = d_mid.astype(bf16)
    low_ref[...] = low
    d_o = right_dot(low, w_ref[...]).astype(bf16)
    do_ref[...] = d_o
    prod = d_o.astype(f32) * o_ref[...].astype(f32)
    half = rows // 2
    for h in range(KEY_VALUE_HEADS):
        ones = [jnp.sum(prod[:, n * 64 : (n + 1) * 64], axis=1, keepdims=True) for n in range(h * GROUP, (h + 1) * GROUP)]
        column = jnp.concatenate([one[half:] for one in ones] + [one[:half] for one in ones], axis=0)
        delta_ref[h : h + 1, :] = jnp.transpose(jnp.broadcast_to(column, (GROUP * rows, 128)))[:1, :]


def middle_call(ints, parts, dy, mid, gain, w, o):
    rows, width = mid.shape
    return call(
        middle_kernel, "middle",
        [shape((rows, width), f32), shape((rows, width)), shape((rows, width)), shape((8, GROUP * rows), f32)],
        [ints, *parts, dy, mid, gain, w, o],
    )


def back_kernel(ints, q_ref, kv_ref, do_ref, lse_ref, delta_ref, qpos_ref, qstart_ref, cos_ref, sin_ref, dq_ref, dkv_ref, qs, ds, ks, vs, dks, dvs, dqs, bias):
    rows, length = do_ref.shape[0], kv_ref.shape[0]
    chunk = CHUNK
    half, part = rows // 2, GROUP * rows // 2
    split_rows(qs, q_ref, rows)
    split_rows(ds, do_ref, rows)
    split_keys(ks, vs, kv_ref)
    kpos = lax.broadcasted_iota(jnp.int32, (length, rows), 0)
    ok = (kpos >= qstart_ref[...]) & (qpos_ref[...] >= kpos)
    allowed = jnp.where(ok, 0.0, NEGATIVE)
    bias[...] = jnp.concatenate([allowed[:, half:]] * GROUP + [allowed[:, :half]] * GROUP, axis=1)

    def head(h, carry):
        lse, delta = lse_ref[pl.ds(h, 1), :], delta_ref[pl.ds(h, 1), :]

        def step(c, dq, columns):
            at = pl.ds(pl.multiple_of(c * chunk, chunk), chunk)
            q, d = qs[h, :columns, :], ds[h, :columns, :]
            k, v = ks[h, at, :], vs[h, at, :]
            p = jnp.exp(right_dot(k, q) + bias[at, :columns] - lse[:, :columns])
            dp = right_dot(v, d)
            low = p.astype(bf16)
            dscore = (p * (dp - delta[:, :columns])).astype(bf16)
            dvs[h, at, :] = plain_dot(low, d)
            dks[h, at, :] = plain_dot(dscore, q)
            return dq + left_dot(k, dscore)

        n = length // chunk
        both = GROUP * rows
        dqs[h] = lax.fori_loop(0, n // 2, functools.partial(step, columns=both), jnp.zeros((64, both), f32), unroll=INNER)
        late = lax.fori_loop(n // 2, n, functools.partial(step, columns=part), jnp.zeros((64, part), f32), unroll=INNER)
        dqs[h, :, :part] = dqs[h, :, :part] + late
        return carry

    lax.fori_loop(0, KEY_VALUE_HEADS, head, 0, unroll=OUTER)
    me = ints[ME]
    own_cos, own_sin = table_rows(cos_ref, ints, me * 2, 2), -table_rows(sin_ref, ints, me * 2, 2)
    scale = HEAD_SIZE**-0.5
    for j in range(8):
        pieces = []
        for n in (2 * j, 2 * j + 1):
            n = min(n, QUERY_HEADS - 1)
            h, g = n // GROUP, n % GROUP
            pieces.append(jnp.concatenate([dqs[h, :, ((1 - late) * GROUP + g) * half : ((1 - late) * GROUP + g + 1) * half] for late in range(2)], axis=1))
        part = jnp.transpose(jnp.concatenate(pieces, axis=0)) * scale
        dq_ref[:, j * 128 : (j + 1) * 128] = rope(part, own_cos, own_sin).astype(bf16)

    def finish(t, carry):
        at = pl.ds(pl.multiple_of(t * 256, 256), 256)
        rows_of = lambda ref, n: jnp.concatenate([half_block(ref.at[n], ints, t * 4 + i) for i in range(4)], axis=0)
        both = [rows_of(dks, n) for n in range(KEY_VALUE_HEADS)] + [rows_of(dvs, n) for n in range(KEY_VALUE_HEADS)]
        both = jnp.concatenate(both, axis=1)
        cos, sin = table_rows(cos_ref, ints, t * 4, 4), -table_rows(sin_ref, ints, t * 4, 4)
        for j, part in enumerate(rope_keys(both, cos, sin)):
            dkv_ref[at, j * 128 : (j + 1) * 128] = part.astype(bf16)
        return carry

    lax.fori_loop(0, length // 256, finish, 0)


def back_call(ints, q, kv, d_o, lse, delta, qpos, qstart, cos, sin):
    rows, length = d_o.shape[0], kv.shape[0]
    both = GROUP * rows
    heads = KEY_VALUE_HEADS
    return call(
        back_kernel, "back",
        [shape((rows, 1024)), shape((length, 2 * KD))],
        [ints, q, kv, d_o, lse, delta, qpos, qstart, cos, sin],
        flops=20e9, read=8e6,
        scratch=[
            pltpu.VMEM((heads, both, 64), bf16),
            pltpu.VMEM((heads, both, 64), bf16),
            pltpu.VMEM((heads, length, 64), bf16),
            pltpu.VMEM((heads, length, 64), bf16),
            pltpu.VMEM((heads, length, 64), f32),
            pltpu.VMEM((heads, length, 64), f32),
            pltpu.VMEM((heads, 64, both), f32),
            pltpu.VMEM((length, both), f32),
        ],
    )


def last_kernel(ints, dq_ref, parts_ref, w_ref, x_ref, gain_ref, dmid_ref, out_ref):
    dkv = add_parts([parts_ref[c] for c in range(parts_ref.shape[0])]).astype(bf16)
    d_ha = right_dot(dkv, w_ref[:, : 2 * KD]) + right_dot(dq_ref[:, :QD], w_ref[:, 2 * KD : 2 * KD + QD])
    x = x_ref[...].astype(f32)
    inv = lax.rsqrt(jnp.mean(x * x, axis=1, keepdims=True) + EPSILON)
    out_ref[...] = (dmid_ref[...] + norm_back(d_ha, x * inv, inv, gain_ref[...])).astype(bf16)


def last_call(ints, dq, parts, w, x, gain, d_mid):
    return call(last_kernel, "last", shape(x.shape), [ints, dq, parts, w, x, gain, d_mid])


def per_device(
    hidden,
    cotangent,
    pairing,
    documents,
    attn_gain,
    w_query,
    w_key,
    w_value,
    w_out,
    mlp_gain,
    w_gate,
    w_up,
    w_down,
):
    rows, width = hidden.shape[2:]
    own = width // 8
    ff = w_gate.shape[1] // 8
    x, y, z, core = (lax.axis_index(name) for name in ("x", "y", "z", "core"))
    me = x * 4 + y
    pairs = pairing.shape[0]
    x_rows = hidden.reshape(rows, width)
    dy = cotangent.reshape(rows, width)

    rows_all = lax.all_gather(x_rows, CTX, axis=0, tiled=True)
    blocks = jnp.stack([pairing, 2 * pairs - 1 - pairing], axis=1).reshape(-1)
    ints = jnp.concatenate([blocks, jnp.stack([x, y, z, core, me, me, me, me]).astype(jnp.int32)])
    shard = jnp.concatenate(
        [w_key, w_value, w_query, attn_gain[:, None], mlp_gain[:, None], jnp.zeros((own, PADDED - 2 * KD - QD - 2), bf16), w_out], axis=1
    )
    w_kvq, out_w, gains = assemble_call(ints, gather_blocks(shard))
    dys = lax.all_gather(after(dy, w_kvq), FSDP, axis=0, tiled=True)
    gain_a, gain_m = gains[:1], gains[1:2]
    positions = seq_positions(pairing, rows)
    docs = documents[:, 0, :]
    own_pos = lax.dynamic_index_in_dim(positions, me, 0)
    own_doc = lax.dynamic_index_in_dim(docs, me, 0)
    start = jnp.sum((docs.reshape(-1, 1) < own_doc).astype(jnp.int32), axis=0, keepdims=True)
    cos, sin = rope_tables(2 * pairs * 64)
    gate_up = jnp.concatenate([w_gate.reshape(own, 8, ff), w_up.reshape(own, 8, ff)], axis=2).transpose(1, 0, 2)
    gate_up = lax.all_to_all(gate_up, FSDP, 0, 0, tiled=True).reshape(width, 2 * ff)
    wg, wu = gate_up[:, :ff], gate_up[:, ff:]
    rows_all, w_kvq, start, out_w = lax.optimization_barrier((rows_all, w_kvq, start, out_w))

    ha_all, kv, q = qkv_call(ints, rows_all, cos, sin, x_rows, w_kvq, gain_a)
    o, lse, mid, hm = attend_call(
        ints, q, kv, own_pos.reshape(-1, 1), start.reshape(-1, 1), x_rows, out_w, gain_m
    )

    dh, dh_its, out, out_its, g_gu, g_down = mlp_call(ints, gather_blocks(hm), dys, wg, wu, w_down)
    dh_parts = send_parts(fold_call(ints, dh, shift(dh_its, "core", 1, 2), width), "z")
    g_gu = lax.all_to_all(g_gu, FSDP, 0, 0, tiled=True)
    mid_in, g_gu = lax.optimization_barrier((mid, g_gu))
    d_mid, low, d_o, delta = middle_call(ints, dh_parts, dy, mid_in, gain_m, out_w, o)

    def by_core(partial):
        view = partial.reshape(4, 2, own, -1)
        return lax.dynamic_index_in_dim(view, core, 1, keepdims=False), lax.dynamic_index_in_dim(view, 1 - core, 1, keepdims=False)

    o_mine, o_its = by_core(left_dot(o, low).astype(bf16))
    d_o, o_its = lax.optimization_barrier((d_o, o_its))
    o_recv = shift(o_its, "core", 1, 2)
    out_recv = shift(after(out_its, d_o), "core", 1, 2)
    g_gu, g_down = lax.psum((g_gu, g_down), "x")

    dq, dkv = back_call(ints, q, kv, d_o, lse, delta, own_pos, start, cos, sin)
    ha_own = lax.dynamic_slice_in_dim(ha_all, me * rows, rows, 0)
    g_kvq = jnp.concatenate([left_dot(ha_all, dkv), left_dot(ha_own, dq[:, :QD])], axis=1).astype(bf16)
    mine, its = by_core(g_kvq)
    turned = turn_call(ints, mine, shift(its, "core", 1, 2), o_mine, after(o_recv, dq))
    g_gu, g_down = after(g_gu, turned[0]), after(g_down, turned[0])
    owners = lax.all_to_all(after(dkv, g_gu).reshape(pairs, rows, 2 * KD), CTX, 0, 0, tiled=True)
    g_gu, g_down = lax.psum((g_gu, g_down), "y")
    z_parts = send_parts(turned, "z")
    out_parts = fold_call(ints, out, after(out_recv, turned[0]), width)
    z_parts[0] = after(z_parts[0], out_parts[0])
    cut = columns_call(ints, z_parts)
    input_grad = last_call(ints, dq, after(owners, cut[0]), w_kvq, x_rows, gain_a, d_mid)
    x_parts = send_parts(cut, "x")
    low_sum = add_parts([after(x_parts[0], input_grad)] + x_parts[1:]).astype(bf16)
    low_sum = add_parts([low_sum] + [shift(low_sum, "y", k) for k in (1, 2, 3)]).astype(bf16)
    *out_parts, _ = lax.optimization_barrier((*out_parts, cut[0]))
    result = (mid + add_parts(send_parts(out_parts, "z"))).astype(bf16)
    g_key, g_value, g_query, g_out, g_gain_a = finish_call(
        ints, [low_sum] + [shift(low_sum, "x", k) for k in (1, 2, 3)], w_key, w_value, w_query, attn_gain[:, None]
    )
    g_gate, g_up, g_down, g_gain_m = spread_call(ints, after(g_gu, low_sum), g_down, w_gate, w_up, mlp_gain[:, None])

    return (
        result.reshape(1, 1, rows, width),
        input_grad.reshape(1, 1, rows, width),
        g_gain_a.reshape(own),
        g_query,
        g_key.T,
        g_value.T,
        g_out,
        g_gain_m.reshape(own),
        g_gate,
        g_up,
        g_down,
    )


def solution(mesh):
    grid = jax.sharding.Mesh(mesh.devices.reshape(4, 4, 4, 2), ("x", "y", "z", "core"))
    tokens = P(CTX, FSDP, None, None)
    vector, matrix = P(FSDP), P(FSDP, None)
    return jax.shard_map(
        per_device,
        mesh=grid,
        in_specs=(tokens, tokens, P(), P(None, FSDP, None), vector, matrix, matrix, matrix, matrix, vector, matrix, matrix, matrix),
        out_specs=(tokens, tokens, vector, matrix, matrix, matrix, matrix, vector, matrix, matrix, matrix),
        check_vma=False,
    )
```
